512 devices in a mesh: img: 8 (over z), seq: 16 (over x, y_hi, core), mdl: 4 (over y_lo).
Axes of the slice: x: 4, y: 8 (y_hi: 2, y_lo: 4; y = y_hi * 4 + y_lo), z: 8, core: 2. Of those that a mesh axis runs over, the one named last changes fastest.
Arguments:
- states: bfloat16 [8, 2048, 3072], P('img', 'seq'), may hold values from -6 to 6
- adjoint: float32 [8, 2048, 3072], P('img', 'seq'), may hold values from -6 to 6
- sampling_step_index: int32 [8], P('img'), may hold values from 0 to 27
- modulated_gain: float32 [3072], replicated, may hold values from 0.1 to 1.9
- query_weight: bfloat16 [3072, 1536], P('seq', 'mdl')
- key_weight: bfloat16 [3072, 1536], P('seq', 'mdl')
- value_weight: bfloat16 [3072, 1536], P('seq', 'mdl'), may hold values from -0.109375 to 0.109375
- output_weight: bfloat16 [1536, 3072], P('mdl', 'seq'), may hold values from -0.15625 to 0.15625
- down_factor: bfloat16 [1536, 64], P('mdl'), may hold values from -0.15625 to 0.15625
- up_factor: bfloat16 [64, 3072], replicated, may hold values from -0.75 to 0.75
Outputs:
- adjoint_drift: float32 [8, 2048, 3072], P('img', 'seq', 'mdl')
- match_residual: float32 [8, 2048, 3072], P('img', 'seq', 'mdl')
- grad_up: float32 [64, 3072], P(None, 'mdl')
- grad_down: float32 [1536, 64], P('mdl')
The draws below stay inside these ranges and needn't reach their ends.
All inputs are finite; a program needn't handle non-finite values.
Results may differ from the reference program's by a relative error of at most 0.0092.
Values may be sent and summed in bfloat16 or wider, within the bound.
No kernel may reach another device: no remote copies, remote signals or barrier semaphores. Data moves between devices by JAX's collectives and lax.ppermute only.
A program may use at most 64 MiB of HBM per device.

```python
import jax
import jax.numpy as jnp
from jax import lax

MODEL_WIDTH = 3072
HEAD_SIZE = 128
LOCAL_HEADS = 12
UPDATE_RANK = 64
STEPS = 28
IMAGES = 8
LENGTH = 2048


def shared_base(key):
    return jax.random.normal(key, (MODEL_WIDTH, LOCAL_HEADS * HEAD_SIZE), jnp.float32)


def draw_query_weight(key, part):
    base = shared_base(key)
    return (base * MODEL_WIDTH ** (-0.5)).astype(jnp.bfloat16)


def draw_key_weight(key, part):
    key = jax.random.fold_in(key, 12)
    own_part = jax.random.normal(key, (MODEL_WIDTH, LOCAL_HEADS * HEAD_SIZE), jnp.float32)
    mixed = own_part
    return (mixed * MODEL_WIDTH ** (-0.5)).astype(jnp.bfloat16)


def with_ends(entries, key, smallest, largest):
    shape = entries.shape
    place = [jax.random.randint(jax.random.fold_in(key, axis), (), 0, shape[axis]) for axis in range(len(shape))]
    entries = entries.at[tuple(place)].set(smallest)
    longest = shape.index(max(shape))
    place[longest] = (place[longest] + 1) % shape[longest]
    return entries.at[tuple(place)].set(largest)


def block_scale(own_key, shape, pieces, low, top_value):
    level, own = 1.0, jax.random.fold_in(own_key, 6)
    for axis_at, blocks in pieces:
        draws = jnp.exp(jax.random.uniform(jax.random.fold_in(own, axis_at), (blocks,), jnp.float32, low / len(pieces), top_value / len(pieces)))
        level = level * jnp.repeat(draws, shape[axis_at] // blocks).reshape([-1 if axis == axis_at else 1 for axis in range(len(shape))])
    return level


def scatter_about(rng, shape, deviation, reach, split=(), kind=jnp.bfloat16):
    values = jax.random.normal(rng, shape, jnp.float32) * deviation
    if len(split) > 0:
        values = block_scale(rng, shape, split, -0.22, 0.18) * values
    return jnp.clip(values, min=-reach, max=reach).astype(kind)


def setup_inputs(seed: int = 0) -> dict:
    streams_of = jax.random.split(jax.random.key(seed), 11)
    return {
        "states": scatter_about(streams_of[0], (IMAGES, LENGTH, MODEL_WIDTH), 1.0, 6.0, ((0, 8), (1, 16))),
        "adjoint": scatter_about(streams_of[1], (IMAGES, LENGTH, MODEL_WIDTH), 1.0, 6.0, ((0, 8), (1, 16)), jnp.float32),
        "sampling_step_index": with_ends(jax.random.randint(streams_of[2], (IMAGES,), 0, STEPS), jax.random.fold_in(streams_of[2], 1), 0, STEPS - 1).astype(jnp.int32),
        "modulated_gain": jnp.clip(1.0 + 0.18 * jax.random.normal(streams_of[3], (MODEL_WIDTH,), jnp.float32), 0.1, 1.9),
        "query_weight": draw_query_weight(jax.random.fold_in(streams_of[10], 71), 0),
        "key_weight": draw_key_weight(jax.random.fold_in(streams_of[10], 71), 0),
        "value_weight": scatter_about(streams_of[6], (MODEL_WIDTH, LOCAL_HEADS * HEAD_SIZE), MODEL_WIDTH ** -0.5, 0.109375, ((0, 16), (1, 4))),
        "output_weight": scatter_about(streams_of[7], (LOCAL_HEADS * HEAD_SIZE, MODEL_WIDTH), (LOCAL_HEADS * HEAD_SIZE) ** -0.5, 0.15625, ((0, 4), (1, 16))),
        "down_factor": scatter_about(streams_of[8], (LOCAL_HEADS * HEAD_SIZE, UPDATE_RANK), (LOCAL_HEADS * HEAD_SIZE) ** -0.5, 0.15625, ((0, 4),)),
        "up_factor": scatter_about(streams_of[9], (UPDATE_RANK, MODEL_WIDTH), UPDATE_RANK ** -0.5, 0.75),
    }


def image_wise(single_states, single_adjoint, single_step, modulated_gain, query_weight, key_weight, value_weight, output_weight, down_factor, up_factor):
    softmax_scale = HEAD_SIZE ** (-0.5)
    contract_axes = (((1,), (1,)), ((), ()))
    leading = (((0,), (0,)), ((), ()))
    inputs = single_states.astype(jnp.float32)
    inverse = lax.rsqrt(lax.optimization_barrier(jnp.mean(inputs * inputs, axis=-1, keepdims=True)) + 1e-06)
    unit_rows = inputs * inverse
    normed = (unit_rows * modulated_gain).astype(jnp.bfloat16)
    queries = jnp.dot(normed, query_weight, preferred_element_type=jnp.float32).astype(jnp.bfloat16)
    key_rows = jnp.dot(normed, key_weight, preferred_element_type=jnp.float32).astype(jnp.bfloat16)
    value_rows = jnp.dot(normed, value_weight, preferred_element_type=jnp.float32).astype(jnp.bfloat16)
    grad_out = lax.dot_general(single_adjoint.astype(jnp.bfloat16), output_weight, contract_axes, preferred_element_type=jnp.float32).astype(jnp.bfloat16)

    def split_heads(matrix):
        return matrix.reshape(matrix.shape[0], LOCAL_HEADS, HEAD_SIZE).transpose(1, 0, 2)

    def per_head(partial_pieces):
        head_query, head_key, head_value, head_grad = partial_pieces
        scores = jnp.dot(head_query, head_key.T, preferred_element_type=jnp.float32) * softmax_scale
        row_max = lax.optimization_barrier(jnp.max(scores, axis=-1, keepdims=True))
        log_total = row_max + jnp.log(lax.optimization_barrier(jnp.sum(jnp.exp(scores - row_max), axis=-1, keepdims=True)))
        attend = jnp.exp(scores - log_total)
        attend_low = attend.astype(jnp.bfloat16)
        output_list = jnp.dot(attend_low, head_value, preferred_element_type=jnp.float32).astype(jnp.bfloat16)
        row_inner = lax.optimization_barrier(jnp.sum(head_grad.astype(jnp.float32) * output_list.astype(jnp.float32), axis=-1, keepdims=True))
        grad_attend = jnp.dot(head_grad, head_value.T, preferred_element_type=jnp.float32)
        grad_scores = (attend * (grad_attend - row_inner)).astype(jnp.bfloat16)
        grad_query = (jnp.dot(grad_scores, head_key, preferred_element_type=jnp.float32) * softmax_scale).astype(jnp.bfloat16)
        grad_key = (jnp.dot(grad_scores.T, head_query, preferred_element_type=jnp.float32) * softmax_scale).astype(jnp.bfloat16)
        grad_value = jnp.dot(attend_low.T, head_grad, preferred_element_type=jnp.float32).astype(jnp.bfloat16)
        return (output_list, grad_query, grad_key, grad_value)
    results = lax.map(per_head, (split_heads(queries), split_heads(key_rows), split_heads(value_rows), split_heads(grad_out)))

    def join_heads(stacked):
        return stacked.transpose(1, 0, 2).reshape(stacked.shape[1], LOCAL_HEADS * HEAD_SIZE)
    output_list, grad_query, grad_key, grad_value = [join_heads(item) for item in results]
    grad_normed = lax.dot_general(grad_query, query_weight, contract_axes, preferred_element_type=jnp.float32)
    grad_normed = grad_normed + lax.dot_general(grad_key, key_weight, contract_axes, preferred_element_type=jnp.float32)
    grad_normed = grad_normed + lax.dot_general(grad_value, value_weight, contract_axes, preferred_element_type=jnp.float32)
    grad_unit = grad_normed * modulated_gain
    inner_rows = lax.optimization_barrier(jnp.mean(grad_unit * unit_rows, axis=-1, keepdims=True))
    adjoint_drift = inverse * (grad_unit - unit_rows * inner_rows)
    time_now = (single_step.astype(jnp.float32) + 1.0) / (STEPS + 1.0)
    noise_level = jnp.sqrt(2.0 * time_now / (1.0 - time_now))
    adjoint_next = single_adjoint + adjoint_drift / STEPS
    rank_update = jnp.dot(output_list, down_factor, preferred_element_type=jnp.float32).astype(jnp.bfloat16)
    drift_difference = jnp.dot(rank_update, up_factor, preferred_element_type=jnp.float32)
    match_residual = 2.0 / noise_level * drift_difference + noise_level * adjoint_next
    scaled_values = (2.0 / noise_level * match_residual).astype(jnp.bfloat16)
    up_term = lax.dot_general(rank_update, scaled_values, leading, preferred_element_type=jnp.float32)
    rank_backward = lax.dot_general(scaled_values, up_factor, contract_axes, preferred_element_type=jnp.float32).astype(jnp.bfloat16)
    down_term = lax.dot_general(output_list, rank_backward, leading, preferred_element_type=jnp.float32)
    return (adjoint_drift, match_residual, up_term, down_term)

def reference(states, adjoint, sampling_step_index, modulated_gain, query_weight, key_weight, value_weight, output_weight, down_factor, up_factor):

    def one_image(partial_pieces):
        return image_wise(partial_pieces[0], partial_pieces[1], partial_pieces[2], modulated_gain, query_weight, key_weight, value_weight, output_weight, down_factor, up_factor)
    adjoint_drift, match_residual, up_terms, down_terms = lax.map(one_image, (states, adjoint, sampling_step_index))
    return (adjoint_drift, match_residual, lax.optimization_barrier(jnp.sum(up_terms, axis=0)), lax.optimization_barrier(jnp.sum(down_terms, axis=0)))
```

```python
import jax
import jax.numpy as jnp
from jax import lax
from jax.experimental import pallas as pl
from jax.experimental.pallas import tpu as pltpu
from jax.sharding import Mesh
from jax.sharding import PartitionSpec as P

MODEL_WIDTH = 3072
HEAD_SIZE = 128
STEPS = 28
SEQ = ("x", "yh", "c")
F32 = jnp.float32
BF16 = jnp.bfloat16
ROWS_T = (((1,), (1,)), ((), ()))
LEADING = (((0,), (0,)), ((), ()))


def swap(value, axis):
    return lax.ppermute(value, axis, [(0, 1), (1, 0)])


def trade(value, axis):
    return lax.all_to_all(value, axis, split_axis=0, concat_axis=0, tiled=True)


def share(value, axis, count):
    return trade(jnp.broadcast_to(value[None], (count,) + value.shape), axis)


def attention_block(query, grad, keys, values):
    scale = HEAD_SIZE ** (-0.5)
    scores = lax.dot_general(query, keys, ROWS_T, preferred_element_type=F32) * scale
    row_max = jnp.max(scores, axis=-1, keepdims=True)
    weights = jnp.exp(scores - row_max)
    attend = weights * (1.0 / jnp.sum(weights, axis=-1, keepdims=True))
    attend_low = attend.astype(BF16)
    outputs = jnp.dot(attend_low, values, preferred_element_type=F32).astype(BF16)
    row_inner = jnp.sum(grad.astype(F32) * outputs.astype(F32), axis=-1, keepdims=True)
    grad_attend = lax.dot_general(grad, values, ROWS_T, preferred_element_type=F32)
    grad_scores = (attend * (grad_attend - row_inner)).astype(BF16)
    grad_query = jnp.dot(grad_scores, keys, preferred_element_type=F32) * scale
    grad_key = lax.dot_general(grad_scores, query, LEADING, preferred_element_type=F32) * scale
    grad_value = lax.dot_general(attend_low, grad, LEADING, preferred_element_type=F32)
    return outputs, grad_query.astype(BF16), grad_key, grad_value


def attention_kernel(q_ref, g_ref, k_ref, v_ref, o_ref, dq_ref, dk_ref, dv_ref):
    keys, values = k_ref[...], v_ref[...]
    size = 256
    for block in range(q_ref.shape[0] // size):
        here = pl.ds(block * size, size)
        outputs, grad_query, grad_key, grad_value = attention_block(
            q_ref[here, :], g_ref[here, :], keys, values
        )
        o_ref[here, :] = outputs
        dq_ref[here, :] = grad_query
        if block == 0:
            dk_ref[...] = grad_key
            dv_ref[...] = grad_value
        else:
            dk_ref[...] += grad_key
            dv_ref[...] += grad_value


def attention(query, grad, keys, values):
    whole = pl.BlockSpec(memory_space=pltpu.VMEM)
    few, many = query.shape, keys.shape
    return pl.pallas_call(
        attention_kernel,
        out_shape=(
            jax.ShapeDtypeStruct(few, BF16),
            jax.ShapeDtypeStruct(few, BF16),
            jax.ShapeDtypeStruct(many, F32),
            jax.ShapeDtypeStruct(many, F32),
        ),
        in_specs=[whole] * 4,
        out_specs=(whole,) * 4,
        compiler_params=pltpu.CompilerParams(vmem_limit_bytes=48 * 1024 * 1024),
        cost_estimate=pl.CostEstimate(
            flops=12 * few[0] * many[0] * few[1],
            bytes_accessed=8 * few[0] * few[1] + 12 * many[0] * many[1],
            transcendentals=few[0] * many[0],
        ),
    )(query, grad, keys, values)


def make_per_device(images, columns, groups, attend):
    def per_device(
        states,
        adjoint,
        sampling_step_index,
        modulated_gain,
        query_weight,
        key_weight,
        value_weight,
        output_weight,
        down_factor,
        up_factor,
    ):
        is_first = lax.axis_index("c") == 0
        low_half = lax.axis_index("yh") == 0
        rows = states.shape[1]
        depth, width = query_weight.shape
        heads = width // HEAD_SIZE
        span = 2 * depth

        def in_order(mine, other, first):
            return jnp.where(first, mine, other), jnp.where(first, other, mine)

        output_t = output_weight.T
        mine, other = in_order(
            jnp.concatenate([query_weight, key_weight], 1),
            jnp.concatenate([output_t, value_weight], 1),
            is_first,
        )
        got = swap(other, "c")
        shard = jnp.concatenate(in_order(mine, got, is_first), 0)
        far_shard = swap(shard, "yh")
        near = share(shard, "x", columns)
        far = share(far_shard, "x", columns)

        inputs = states[0].astype(F32)
        inverse = lax.rsqrt(jnp.mean(inputs * inputs, axis=-1, keepdims=True) + 1e-06)
        unit_rows = inputs * inverse
        normed = (unit_rows * modulated_gain).astype(BF16)
        adjoint_low = adjoint[0].astype(BF16)
        chip_normed = jnp.concatenate(in_order(normed, swap(normed, "c"), is_first), 0)
        far_adjoint = lax.ppermute(adjoint_low, "c", [(0, 1)])
        chip_adjoint = jnp.concatenate([far_adjoint, adjoint_low], 0)
        left = jnp.where(is_first, chip_normed, chip_adjoint)

        def halves(matrix):
            cut = matrix.reshape(2 * rows, columns, 2, span)
            return [
                part.reshape(2 * rows, columns * span)
                for part in in_order(cut[:, :, 0], cut[:, :, 1], low_half)
            ]

        flat_near, flat_far = (w.reshape(columns * span, 2 * width) for w in (near, far))

        def project(matrix, first, last):
            near_part, far_part = halves(matrix)
            total = jnp.dot(near_part, flat_near[:, first:last], preferred_element_type=F32)
            total = total + jnp.dot(far_part, flat_far[:, first:last], preferred_element_type=F32)
            return total.astype(BF16)

        def by_head(matrix):
            split = matrix.reshape(2 * rows, heads, HEAD_SIZE).transpose(1, 0, 2)
            return jnp.pad(split, ((0, columns - heads), (0, 0), (0, 0)))

        both = jnp.stack(
            [by_head(project(left, 0, width)), by_head(project(chip_normed, width, 2 * width))], 1
        )
        both = trade(both, "x")
        key_like = both[:, 1].reshape(columns * 2 * rows, HEAD_SIZE)
        query_like = both[:, 0].reshape(columns, 2, rows, HEAD_SIZE)
        keep, give = in_order(query_like[:, 0], query_like[:, 1], is_first)
        flat = (columns * rows, HEAD_SIZE)
        keep, give = keep.reshape(flat), give.reshape(flat)
        far_like = swap(key_like, "yh")
        query, grad = in_order(keep, swap(give, "c"), is_first)
        near_key, near_value = in_order(key_like, swap(key_like, "c"), is_first)
        far_key, far_value = in_order(far_like, swap(far_like, "c"), is_first)
        keys = jnp.concatenate([near_key, far_key], 0)
        values = jnp.concatenate([near_value, far_value], 0)
        outputs, grad_query, grad_key, grad_value = attend(query, grad, keys, values)

        block = (columns, rows, HEAD_SIZE)
        early = trade(jnp.stack([outputs.reshape(block), grad_query.reshape(block)], 1), "x")

        def sum_parts(part):
            cut = part.reshape(2, columns, 2, rows, HEAD_SIZE)
            stay, leave = in_order(cut[:, :, 0], cut[:, :, 1], is_first)
            total = stay + swap(leave.astype(BF16), "c").astype(F32)
            return total[0] + swap(total[1].astype(BF16), "yh").astype(F32)

        late = jnp.stack([sum_parts(grad_key), sum_parts(grad_value)], 1).astype(BF16)
        late = trade(late, "x")

        def by_token(pieces):
            return pieces[:heads].transpose(1, 0, 2).reshape(rows, width)

        outputs, grad_query = by_token(early[:, 0]), by_token(early[:, 1])
        grad_key, grad_value = by_token(late[:, 0]), by_token(late[:, 1])

        rank_part = jnp.dot(outputs, down_factor, preferred_element_type=F32)
        rank_update = jnp.sum(share(rank_part, "mdl", groups), axis=0).astype(BF16)

        near_other, far_other = swap(near, "c"), swap(far, "c")
        zero = jnp.zeros_like(grad_query)
        own_side = jnp.concatenate(
            [jnp.where(is_first, grad_query, zero), jnp.where(is_first, grad_key, grad_value)], 1
        )
        other_side = jnp.concatenate(
            [jnp.where(is_first, zero, grad_query), jnp.where(is_first, grad_value, grad_key)], 1
        )

        def pull(own_weight, other_weight):
            return jnp.einsum(
                "tc,xfc->xtf", own_side, own_weight, preferred_element_type=F32
            ) + jnp.einsum("tc,xfc->xtf", other_side, other_weight, preferred_element_type=F32)

        partial_grad = jnp.concatenate(
            in_order(pull(near, near_other), pull(far, far_other), low_half), 2
        )
        local_width = MODEL_WIDTH // groups

        def by_group(matrix):
            return matrix.reshape(matrix.shape[0], groups, local_width).transpose(1, 0, 2)

        gain_groups = modulated_gain.reshape(groups, 1, local_width)
        grad_unit_part = partial_grad * gain_groups
        inner_part = jnp.sum(grad_unit_part * by_group(unit_rows), axis=(0, 2))[:, None]
        rank_grad_part = jnp.einsum(
            "mtf,mrf->tr",
            grad_unit_part.astype(BF16),
            by_group(up_factor),
            preferred_element_type=F32,
        )
        inner_high = inner_part.astype(BF16)
        inner_low = (inner_part - inner_high.astype(F32)).astype(BF16)
        rank = up_factor.shape[0]
        extra = jnp.concatenate(
            [
                rank_grad_part.astype(BF16),
                inner_high,
                inner_low,
                jnp.zeros((rows, HEAD_SIZE - rank - 2), BF16),
            ],
            1,
        )
        parcel = jnp.concatenate(
            [
                grad_unit_part.astype(BF16),
                jnp.broadcast_to(extra[None], (groups, rows, HEAD_SIZE)),
            ],
            2,
        )
        summed = jnp.sum(trade(parcel, "mdl").astype(F32), axis=0)
        grad_unit = summed[:, :local_width]
        rank_grad = summed[:, local_width : local_width + rank]
        inner_rows = jnp.sum(
            summed[:, local_width + rank : local_width + rank + 2], axis=-1, keepdims=True
        )
        inner_rows = inner_rows / MODEL_WIDTH

        first_column = lax.axis_index("mdl") * local_width
        unit_share = lax.dynamic_slice_in_dim(unit_rows, first_column, local_width, 1)
        adjoint_share = lax.dynamic_slice_in_dim(adjoint[0], first_column, local_width, 1)
        up_portion = lax.dynamic_slice_in_dim(up_factor, first_column, local_width, 1)
        adjoint_drift = inverse * (grad_unit - unit_share * inner_rows)
        time_now = (sampling_step_index[0].astype(F32) + 1.0) / (STEPS + 1.0)
        noise_level = jnp.sqrt(2.0 * time_now / (1.0 - time_now))
        adjoint_next = adjoint_share + adjoint_drift / STEPS
        drift_difference = jnp.dot(rank_update, up_portion, preferred_element_type=F32)
        match_residual = 2.0 / noise_level * drift_difference + noise_level * adjoint_next
        scaled_values = (2.0 / noise_level * match_residual).astype(BF16)
        up_term = lax.dot_general(rank_update, scaled_values, LEADING, preferred_element_type=F32)

        up_square = lax.dot_general(up_factor, up_factor, ROWS_T, preferred_element_type=F32)
        adjoint_rank = lax.dot_general(adjoint_low, up_factor, ROWS_T, preferred_element_type=F32)
        unit_rank = lax.dot_general(
            unit_rows.astype(BF16), up_factor, ROWS_T, preferred_element_type=F32
        )
        update_rank = jnp.dot(
            rank_update.astype(F32), up_square, precision=lax.Precision.HIGHEST
        )
        drift_rank = inverse * (rank_grad - unit_rank * inner_rows)
        ratio = 2.0 / noise_level
        rank_backward = ratio * ratio * update_rank + 2.0 * (adjoint_rank + drift_rank / STEPS)
        down_term = lax.dot_general(
            rank_backward.astype(BF16), outputs, LEADING, preferred_element_type=F32
        )

        cuts = 4
        pieces = columns * 4
        table = jnp.concatenate([up_term, down_term, jnp.zeros((rank, width), F32)], 1)
        table = table.astype(BF16).reshape(cuts, rank // cuts, cuts, width)
        table = table.transpose(0, 2, 1, 3).reshape(pieces, rank // cuts, width)
        piece = jnp.sum(trade(table, SEQ).astype(F32), axis=0)
        piece = jnp.sum(share(piece, "img", images), axis=0).astype(BF16)
        table = share(piece, SEQ, pieces).astype(F32)
        table = table.reshape(cuts, cuts, rank // cuts, width).transpose(0, 2, 1, 3)
        table = table.reshape(rank, cuts * width)
        grad_up = table[:, :local_width]
        grad_down = table[:, local_width : local_width + width].T
        return (adjoint_drift[None], match_residual[None], grad_up, grad_down)

    return per_device


def build(mesh, attend=attention):
    images, seq, groups = (mesh.shape[name] for name in ("img", "seq", "mdl"))
    columns = seq // 4
    cut = Mesh(
        mesh.devices.reshape(images, columns, 2, 2, groups), ("img", "x", "yh", "c", "mdl")
    )
    return jax.shard_map(
        make_per_device(images, columns, groups, attend),
        mesh=cut,
        in_specs=(
            P("img", SEQ, None),
            P("img", SEQ, None),
            P("img"),
            P(),
            P(SEQ, "mdl"),
            P(SEQ, "mdl"),
            P(SEQ, "mdl"),
            P("mdl", SEQ),
            P("mdl", None),
            P(),
        ),
        out_specs=(P("img", SEQ, "mdl"), P("img", SEQ, "mdl"), P(None, "mdl"), P("mdl", None)),
        check_vma=False,
    )


def solution(mesh):
    return build(mesh)
```

```python
import jax
import jax.numpy as jnp
from jax import lax
from jax.experimental import pallas as pl
from jax.experimental.pallas import tpu as pltpu
from jax.sharding import Mesh
from jax.sharding import PartitionSpec as P

MODEL_WIDTH = 3072
HEAD_SIZE = 128
STEPS = 28
SEQ = ("x", "yh", "c")
F32 = jnp.float32
BF16 = jnp.bfloat16
ROWS_T = (((1,), (1,)), ((), ()))
LEADING = (((0,), (0,)), ((), ()))


def swap(value, axis):
    return lax.ppermute(value, axis, [(0, 1), (1, 0)])


def trade(value, axis):
    return lax.all_to_all(value, axis, split_axis=0, concat_axis=0, tiled=True)


def share(value, axis, count):
    return trade(jnp.broadcast_to(value[None], (count,) + value.shape), axis)


def attention_block(query, grad, keys, values):
    scale = HEAD_SIZE ** (-0.5)
    scores = lax.dot_general(query, keys, ROWS_T, preferred_element_type=F32) * scale
    row_max = jnp.max(scores, axis=-1, keepdims=True)
    weights = jnp.exp(scores - row_max)
    attend = weights * (1.0 / jnp.sum(weights, axis=-1, keepdims=True))
    attend_low = attend.astype(BF16)
    outputs = jnp.dot(attend_low, values, preferred_element_type=F32).astype(BF16)
    row_inner = jnp.sum(grad.astype(F32) * outputs.astype(F32), axis=-1, keepdims=True)
    grad_attend = lax.dot_general(grad, values, ROWS_T, preferred_element_type=F32)
    grad_scores = (attend * (grad_attend - row_inner)).astype(BF16)
    grad_query = jnp.dot(grad_scores, keys, preferred_element_type=F32) * scale
    grad_key = lax.dot_general(grad_scores, query, LEADING, preferred_element_type=F32) * scale
    grad_value = lax.dot_general(attend_low, grad, LEADING, preferred_element_type=F32)
    return outputs, grad_query.astype(BF16), grad_key, grad_value


def project_kernel(
    place_ref, near_ref, far_ref, rows_ref, rows_in_ref, _, out_ref, total_one, total_two
):
    step = pl.program_id(0)
    first, half = place_ref[0] == 0, place_ref[1]
    _, span, both = near_ref.shape
    width = both // 2

    def terms(side, weight):
        here = pl.ds(pl.multiple_of((2 * step + side) * span, HEAD_SIZE), span)
        own, other = rows_ref[0, :, here], rows_in_ref[0, :, here]
        rows = jnp.concatenate([jnp.where(first, own, other), jnp.where(first, other, own)], 0)
        adjoint = jnp.concatenate([rows_in_ref[1, :, here], rows_ref[1, :, here]], 0)
        left = jnp.where(first, rows, adjoint)
        return (
            jnp.dot(left, weight[:, :width], preferred_element_type=F32),
            jnp.dot(rows, weight[:, width:], preferred_element_type=F32),
        )

    near_one, near_two = terms(half, near_ref[0])
    far_one, far_two = terms(1 - half, far_ref[0])

    @pl.when(step == 0)
    def _():
        total_one[...] = near_one + far_one
        total_two[...] = near_two + far_two

    @pl.when(step > 0)
    def _():
        total_one[...] += near_one + far_one
        total_two[...] += near_two + far_two

    @pl.when(step == pl.num_programs(0) - 1)
    def _():
        chips, _, cores, rows, _ = out_ref.shape
        for kind, total in enumerate((total_one, total_two)):
            low = total[...].astype(BF16)
            for chip in range(chips):
                columns = slice(chip * HEAD_SIZE, (chip + 1) * HEAD_SIZE)
                for core in range(cores):
                    if chip * HEAD_SIZE < width:
                        piece = low[core * rows : (core + 1) * rows, columns]
                    else:
                        piece = jnp.zeros((rows, HEAD_SIZE), BF16)
                    out_ref[chip, kind, core] = piece


def project(place, near, far, rows_own, rows_in, held):
    _, rows, features = rows_own.shape
    chips, span, both = far.shape
    whole = pl.BlockSpec((2, rows, features), lambda i: (0, 0, 0))
    block = pl.BlockSpec((1, span, both), lambda i: (i, 0, 0))
    shape = (chips, 2, 2, rows, HEAD_SIZE)
    return pl.pallas_call(
        project_kernel,
        grid=(chips,),
        out_shape=jax.ShapeDtypeStruct(shape, BF16),
        in_specs=[pl.BlockSpec(memory_space=pltpu.SMEM), block, block, whole, whole]
        + [pl.BlockSpec(memory_space=pl.ANY)],
        out_specs=pl.BlockSpec(shape, lambda i: (0, 0, 0, 0, 0)),
        scratch_shapes=[pltpu.VMEM((2 * rows, both // 2), F32)] * 2,
        compiler_params=pltpu.CompilerParams(vmem_limit_bytes=32 * 1024 * 1024),
        cost_estimate=pl.CostEstimate(
            flops=8 * rows * chips * span * both,
            bytes_accessed=4 * chips * span * both + 8 * rows * features,
            transcendentals=0,
        ),
    )(place, near, far, rows_own, rows_in, held)


def attention_kernel(
    core_ref, both_ref, both_in_ref, far_ref, far_in_ref, _,
    early_ref, leave_ref, stay_ref, key_sum, value_sum,
):
    core = core_ref[0]
    first = core == 0
    blocks, _, _, rows, size = both_ref.shape
    count = blocks * rows
    near_ref, near_in_ref = both_ref.at[:, 1], both_in_ref.at[:, 1]

    def flat(value):
        return value.reshape(count, size)

    def in_order(mine, other):
        return jnp.where(first, mine, other), jnp.where(first, other, mine)

    query, grad = in_order(flat(both_ref[:, 0, core]), flat(both_in_ref[:, 0, core]))
    pairs = [
        in_order(flat(mine[:, of]), flat(theirs[:, of]))
        for mine, theirs in ((near_ref, near_in_ref), (far_ref, far_in_ref))
        for of in (core, 1 - core)
    ]
    keys = jnp.concatenate([pair[0] for pair in pairs], 0)
    values = jnp.concatenate([pair[1] for pair in pairs], 0)
    part = 2 * rows
    for block in range(count // part):
        here = slice(block * part, (block + 1) * part)
        outputs, grad_query, grad_key, grad_value = attention_block(
            query[here], grad[here], keys, values
        )
        cut = (2, rows, size)
        early_ref[2 * block : 2 * block + 2, 0] = outputs.reshape(cut)
        early_ref[2 * block : 2 * block + 2, 1] = grad_query.reshape(cut)
        if block == 0:
            key_sum[...] = grad_key
            value_sum[...] = grad_value
        else:
            key_sum[...] += grad_key
            value_sum[...] += grad_value
    for kind, total in enumerate((key_sum, value_sum)):
        for side in range(2):
            own = pl.ds(2 * side * count, count)
            other = pl.ds((2 * side + 1) * count, count)
            stay_ref[side, :, kind] = total[own, :].reshape(blocks, rows, size)
            leave_ref[side, :, kind] = total[other, :].reshape(blocks, rows, size).astype(BF16)


def attention(core, held, *operands):
    whole = pl.BlockSpec(memory_space=pltpu.VMEM)
    blocks, _, _, rows, size = operands[0].shape
    queries, keys = blocks * rows, 4 * blocks * rows
    return pl.pallas_call(
        attention_kernel,
        out_shape=(
            jax.ShapeDtypeStruct((blocks, 2, rows, size), BF16),
            jax.ShapeDtypeStruct((2, blocks, 2, rows, size), BF16),
            jax.ShapeDtypeStruct((2, blocks, 2, rows, size), F32),
        ),
        in_specs=[pl.BlockSpec(memory_space=pltpu.SMEM)]
        + [whole] * len(operands)
        + [pl.BlockSpec(memory_space=pl.ANY)],
        out_specs=(whole,) * 3,
        scratch_shapes=[pltpu.VMEM((keys, size), F32)] * 2,
        compiler_params=pltpu.CompilerParams(vmem_limit_bytes=40 * 1024 * 1024),
        cost_estimate=pl.CostEstimate(
            flops=12 * queries * keys * size,
            bytes_accessed=8 * queries * size + 10 * keys * size,
            transcendentals=queries * keys,
        ),
    )(core, *operands, held)


def pull_kernel(
    place_ref, back_ref, down_ref,
    near_ref, far_ref, near_in_ref, far_in_ref,
    states_ref, inverse_ref, gain_ref, up_ref, parcel_ref, inner_sum, rank_sum,
):
    step = pl.program_id(0)
    groups, rows, _ = parcel_ref.shape
    width = gain_ref.shape[1]
    head_width = near_ref.shape[2] // 2
    heads = head_width // HEAD_SIZE
    first, low_half = place_ref[0] == 0, place_ref[1] == 0

    outputs, grad_query, grad_key, grad_value = [
        jnp.concatenate([back_ref[head, kind] for head in range(heads)], 1) for kind in range(4)
    ]
    own = jnp.where(first, grad_key, grad_value)
    other = jnp.where(first, grad_value, grad_key)

    def times(rows_in, weight):
        return lax.dot_general(rows_in, weight, ROWS_T, preferred_element_type=F32)

    def pull(mine, theirs):
        query_weight = jnp.where(first, mine[0, :, :head_width], theirs[0, :, :head_width])
        total = times(grad_query, query_weight)
        total = total + times(own, mine[0, :, head_width:])
        return total + times(other, theirs[0, :, head_width:])

    near = pull(near_ref, near_in_ref)
    far = pull(far_ref, far_in_ref)
    part = jnp.concatenate(
        [jnp.where(low_half, near, far), jnp.where(low_half, far, near)], 1
    )
    part = part * gain_ref[...]
    unit = states_ref[...].astype(F32) * inverse_ref[...]
    inner = jnp.sum(part * unit, axis=-1, keepdims=True)
    part = part.astype(BF16)
    rank = times(part, up_ref[...])
    parcel_ref[step, :, :width] = part

    @pl.when(step == 0)
    def _():
        inner_sum[...] = inner
        rank_sum[...] = rank

    @pl.when(step > 0)
    def _():
        inner_sum[...] += inner
        rank_sum[...] += rank

    @pl.when(step == groups - 1)
    def _():
        total = inner_sum[...]
        high = total.astype(BF16).astype(F32)
        lane = lax.broadcasted_iota(jnp.int32, rank_sum.shape, 1)
        extra = jnp.where(lane == HEAD_SIZE - 2, high, rank_sum[...])
        extra = jnp.where(lane == HEAD_SIZE - 1, total - high, extra).astype(BF16)
        low_rank = jnp.dot(outputs, down_ref[...], preferred_element_type=F32)
        low_high = low_rank.astype(BF16).astype(F32)
        rest = low_rank - low_high
        low_pair = jnp.where(lane < HEAD_SIZE // 2, low_high, rest).astype(BF16)
        for group in range(groups):
            parcel_ref[group, :, width : width + HEAD_SIZE] = extra
            parcel_ref[group, :, width + HEAD_SIZE :] = low_pair


def pull_back(place, back, down_twice, weights, states, inverse, gain, up_padded):
    groups, span, both = weights[0].shape
    rows, features = states.shape
    width = features // groups
    whole = pl.BlockSpec(memory_space=pltpu.VMEM)
    return pl.pallas_call(
        pull_kernel,
        grid=(groups,),
        out_shape=jax.ShapeDtypeStruct((groups, rows, width + 2 * HEAD_SIZE), BF16),
        in_specs=[
            pl.BlockSpec(memory_space=pltpu.SMEM),
            pl.BlockSpec(back.shape, lambda i: (0, 0, 0, 0)),
            pl.BlockSpec(down_twice.shape, lambda i: (0, 0)),
        ]
        + [pl.BlockSpec((1,) + weight.shape[1:], lambda i: (i, 0, 0)) for weight in weights]
        + [
            pl.BlockSpec((rows, width), lambda i: (0, i)),
            pl.BlockSpec((rows, 1), lambda i: (0, 0)),
            pl.BlockSpec((1, width), lambda i: (0, i)),
            pl.BlockSpec((HEAD_SIZE, width), lambda i: (0, i)),
        ],
        out_specs=pl.BlockSpec((groups, rows, width + 2 * HEAD_SIZE), lambda i: (0, 0, 0)),
        scratch_shapes=[pltpu.VMEM((rows, 1), F32), pltpu.VMEM((rows, HEAD_SIZE), F32)],
        compiler_params=pltpu.CompilerParams(vmem_limit_bytes=56 * 1024 * 1024),
        cost_estimate=pl.CostEstimate(
            flops=3 * rows * both * features,
            bytes_accessed=4 * features * both,
            transcendentals=0,
        ),
    )(place, back, down_twice, *weights, states, inverse, gain.reshape(1, features), up_padded)


def make_per_device(images, columns, groups):
    def per_device(
        states,
        adjoint,
        sampling_step_index,
        modulated_gain,
        query_weight,
        key_weight,
        value_weight,
        output_weight,
        down_factor,
        up_factor,
    ):
        is_first = lax.axis_index("c") == 0
        rows = states.shape[1]
        width = query_weight.shape[1]
        heads = width // HEAD_SIZE

        def in_order(mine, other, first):
            return jnp.where(first, mine, other), jnp.where(first, other, mine)

        mine, other = in_order(
            jnp.concatenate([query_weight, key_weight], 1),
            jnp.concatenate([output_weight.T, value_weight], 1),
            is_first,
        )
        shard = jnp.concatenate(in_order(mine, swap(other, "c"), is_first), 0)
        far_shard = swap(shard, "yh")
        near = share(shard, "x", columns)

        inputs = states[0].astype(F32)
        inverse = lax.rsqrt(jnp.mean(inputs * inputs, axis=-1, keepdims=True) + 1e-06)
        unit_rows = inputs * inverse
        normed = (unit_rows * modulated_gain).astype(BF16)
        adjoint_low = adjoint[0].astype(BF16)
        place = jnp.stack([lax.axis_index("c"), lax.axis_index("yh")]).astype(jnp.int32)
        rows_own = jnp.stack([normed, adjoint_low])
        rows_in = swap(rows_own, "c")
        far = share(far_shard, "x", columns)
        near_in, far_in = swap(near, "c"), swap(far, "c")

        both = trade(project(place, near, far, rows_own, rows_in, near_in), "x")
        far_like = swap(both[:, 1], "yh")
        early, leave, stay = attention(
            place, far_in, both, swap(both, "c"), far_like, swap(far_like, "c")
        )

        stay = stay + swap(leave, "c").astype(F32)
        late = stay[0] + swap(stay[1].astype(BF16), "yh").astype(F32)
        back = trade(jnp.concatenate([early, late.astype(BF16)], 1), "x")
        outputs = back[:heads, 0].transpose(1, 0, 2).reshape(rows, width)

        weights = (near, far, near_in, far_in)
        rank = up_factor.shape[0]
        up_padded = jnp.pad(up_factor, ((0, HEAD_SIZE - rank), (0, 0)))
        down_twice = jnp.concatenate([down_factor, down_factor], 1)
        local_width = MODEL_WIDTH // groups
        parcel = pull_back(
            place, back, down_twice, weights, states[0], inverse, modulated_gain, up_padded
        )
        summed = jnp.sum(trade(parcel, "mdl").astype(F32), axis=0)
        grad_unit = summed[:, :local_width]
        rank_grad = summed[:, local_width : local_width + rank]
        pair = summed[:, local_width + HEAD_SIZE - 2 : local_width + HEAD_SIZE]
        inner_rows = jnp.sum(pair, axis=-1, keepdims=True) / MODEL_WIDTH
        high = local_width + HEAD_SIZE
        rest = high + rank
        rank_update = (summed[:, high : high + rank] + summed[:, rest : rest + rank]).astype(BF16)

        first_column = lax.axis_index("mdl") * local_width
        unit_share = lax.dynamic_slice_in_dim(unit_rows, first_column, local_width, 1)
        adjoint_share = lax.dynamic_slice_in_dim(adjoint[0], first_column, local_width, 1)
        up_portion = lax.dynamic_slice_in_dim(up_factor, first_column, local_width, 1)
        adjoint_drift = inverse * (grad_unit - unit_share * inner_rows)
        time_now = (sampling_step_index[0].astype(F32) + 1.0) / (STEPS + 1.0)
        noise_level = jnp.sqrt(2.0 * time_now / (1.0 - time_now))
        adjoint_next = adjoint_share + adjoint_drift / STEPS
        drift_difference = jnp.dot(rank_update, up_portion, preferred_element_type=F32)
        match_residual = 2.0 / noise_level * drift_difference + noise_level * adjoint_next
        scaled_values = (2.0 / noise_level * match_residual).astype(BF16)
        up_term = lax.dot_general(rank_update, scaled_values, LEADING, preferred_element_type=F32)

        up_square = lax.dot_general(up_factor, up_factor, ROWS_T, preferred_element_type=F32)
        adjoint_rank = lax.dot_general(adjoint_low, up_factor, ROWS_T, preferred_element_type=F32)
        unit_rank = lax.dot_general(
            unit_rows.astype(BF16), up_factor, ROWS_T, preferred_element_type=F32
        )
        update_rank = jnp.dot(
            rank_update.astype(F32), up_square, precision=lax.Precision.HIGHEST
        )
        drift_rank = inverse * (rank_grad - unit_rank * inner_rows)
        ratio = 2.0 / noise_level
        rank_backward = ratio * ratio * update_rank + 2.0 * (adjoint_rank + drift_rank / STEPS)
        down_term = lax.dot_general(
            rank_backward.astype(BF16), outputs, LEADING, preferred_element_type=F32
        )

        pieces = columns * 2
        table = jnp.concatenate([up_term, down_term], 1).astype(BF16)
        table = table.reshape(pieces, rank // pieces, local_width + width)
        piece = jnp.sum(trade(table, ("x", "c")).astype(F32), axis=0).astype(BF16)
        piece = share(piece, "img", images).astype(F32)
        piece = jnp.sum(piece, axis=0).astype(BF16)
        table = share(piece, SEQ, 2 * pieces).astype(F32)
        table = jnp.sum(table.reshape(columns, 2, 2, rank // pieces, -1), axis=1)
        table = table.reshape(rank, local_width + width)
        grad_up = table[:, :local_width]
        grad_down = table[:, local_width : local_width + width].T
        return (adjoint_drift[None], match_residual[None], grad_up, grad_down)

    return per_device


def build(mesh):
    images, seq, groups = (mesh.shape[name] for name in ("img", "seq", "mdl"))
    columns = seq // 4
    cut = Mesh(
        mesh.devices.reshape(images, columns, 2, 2, groups), ("img", "x", "yh", "c", "mdl")
    )
    return jax.shard_map(
        make_per_device(images, columns, groups),
        mesh=cut,
        in_specs=(
            P("img", SEQ, None),
            P("img", SEQ, None),
            P("img"),
            P(),
            P(SEQ, "mdl"),
            P(SEQ, "mdl"),
            P(SEQ, "mdl"),
            P("mdl", SEQ),
            P("mdl", None),
            P(),
        ),
        out_specs=(P("img", SEQ, "mdl"), P("img", SEQ, "mdl"), P(None, "mdl"), P("mdl", None)),
        check_vma=False,
    )


def solution(mesh):
    return build(mesh)
```

```python
import jax
import jax.numpy as jnp
from jax import lax
from jax.experimental import pallas as pl
from jax.experimental.pallas import tpu as pltpu
from jax.sharding import Mesh
from jax.sharding import PartitionSpec as P

MODEL_WIDTH = 3072
HEAD_SIZE = 128
STEPS = 28
SEQ = ("x", "yh", "c")
F32 = jnp.float32
BF16 = jnp.bfloat16
ROWS_T = (((1,), (1,)), ((), ()))
LEADING = (((0,), (0,)), ((), ()))


def swap(value, axis):
    return lax.ppermute(value, axis, [(0, 1), (1, 0)])


def trade(value, axis):
    return lax.all_to_all(value, axis, split_axis=0, concat_axis=0, tiled=True)


def share(value, axis, count):
    return trade(jnp.broadcast_to(value[None], (count,) + value.shape), axis)


def attention_block(query, grad, keys, values):
    scale = HEAD_SIZE ** (-0.5)
    scores = lax.dot_general(query, keys, ROWS_T, preferred_element_type=F32) * scale
    row_max = jnp.max(scores, axis=-1, keepdims=True)
    weights = jnp.exp(scores - row_max)
    attend = weights * (1.0 / jnp.sum(weights, axis=-1, keepdims=True))
    attend_low = attend.astype(BF16)
    outputs = jnp.dot(attend_low, values, preferred_element_type=F32).astype(BF16)
    row_inner = jnp.sum(grad.astype(F32) * outputs.astype(F32), axis=-1, keepdims=True)
    grad_attend = lax.dot_general(grad, values, ROWS_T, preferred_element_type=F32)
    grad_scores = (attend * (grad_attend - row_inner)).astype(BF16)
    grad_query = jnp.dot(grad_scores, keys, preferred_element_type=F32) * scale
    grad_key = lax.dot_general(grad_scores, query, LEADING, preferred_element_type=F32) * scale
    grad_value = lax.dot_general(attend_low, grad, LEADING, preferred_element_type=F32)
    return outputs, grad_query.astype(BF16), grad_key, grad_value


def pack_kernel(place_ref, query_ref, key_ref, output_ref, value_ref, mine_ref, other_ref):
    first, even = place_ref[0] == 0, place_ref[2] == 0
    left = jnp.where(even, query_ref[...], key_ref[...])
    right = jnp.where(even, output_ref[...], value_ref[...])
    mine_ref[...] = jnp.where(first, left, right)
    other_ref[...] = jnp.where(first, right, left)


def pack(place, *weights):
    whole = pl.BlockSpec(memory_space=pltpu.VMEM)
    shape = jax.ShapeDtypeStruct(weights[0].shape, BF16)
    return pl.pallas_call(
        pack_kernel,
        out_shape=(shape, shape),
        in_specs=[pl.BlockSpec(memory_space=pltpu.SMEM)] + [whole] * len(weights),
        out_specs=(whole, whole),
        compiler_params=pltpu.CompilerParams(vmem_limit_bytes=56 * 1024 * 1024),
        cost_estimate=pl.CostEstimate(
            flops=0, bytes_accessed=12 * weights[0].size, transcendentals=0
        ),
    )(place, *weights)


def project_kernel(
    place_ref, near_ref, near_up_ref, near_down_ref, far_ref, far_up_ref, far_down_ref,
    rows_ref, rows_in_ref, out_ref, weights_ref, total, total_other,
):
    step = pl.program_id(0)
    first, half, even = place_ref[0] == 0, place_ref[1], place_ref[2] == 0
    _, span, width = near_ref.shape

    def in_order(mine, other):
        return jnp.where(even, mine, other), jnp.where(even, other, mine)

    def left(side):
        here = pl.ds(pl.multiple_of((2 * step + side) * span, HEAD_SIZE), span)
        own, other = rows_ref[0, :, here], rows_in_ref[0, :, here]
        rows = jnp.concatenate([jnp.where(first, own, other), jnp.where(first, other, own)], 0)
        adjoint = jnp.concatenate([rows_in_ref[1, :, here], rows_ref[1, :, here]], 0)
        return in_order(jnp.where(first, rows, adjoint), rows)

    near = near_ref[0], jnp.concatenate([near_up_ref[0], near_down_ref[0]], 0)
    far = far_ref[0], jnp.concatenate([far_up_ref[0], far_down_ref[0]], 0)
    for side, weights in enumerate((near, far)):
        one, two = in_order(*weights)
        weights_ref[side, 0, :, :width] = one
        weights_ref[side, 0, :, width:] = two
    near_left, far_left = left(half), left(1 - half)
    term, term_other = [
        jnp.dot(
            jnp.concatenate([near_left[kind], far_left[kind]], 1),
            jnp.concatenate([near[kind], far[kind]], 0),
            preferred_element_type=F32,
        )
        for kind in range(2)
    ]

    @pl.when(step == 0)
    def _():
        total[...] = term
        total_other[...] = term_other

    @pl.when(step > 0)
    def _():
        total[...] += term
        total_other[...] += term_other

    @pl.when(step == pl.num_programs(0) - 1)
    def _():
        chips, _, cores, rows, _ = out_ref.shape
        for kind, sums in enumerate(in_order(total[...], total_other[...])):
            low = sums.astype(BF16)
            for chip in range(chips):
                columns = slice(chip * HEAD_SIZE, (chip + 1) * HEAD_SIZE)
                for core in range(cores):
                    if chip * HEAD_SIZE < width:
                        piece = low[core * rows : (core + 1) * rows, columns]
                    else:
                        piece = jnp.zeros((rows, HEAD_SIZE), BF16)
                    out_ref[chip, kind, core] = piece


def project(place, near, far, rows_own, rows_in):
    _, rows, features = rows_own.shape
    chips, span, width = far[0].shape
    whole = pl.BlockSpec((2, rows, features), lambda i: (0, 0, 0))
    shape = (chips, 2, 2, rows, HEAD_SIZE)
    weights = jax.ShapeDtypeStruct((2, chips, span, 2 * width), BF16)
    weights_block = pl.BlockSpec((2, 1, span, 2 * width), lambda i: (0, i, 0, 0))
    return pl.pallas_call(
        project_kernel,
        grid=(chips,),
        out_shape=(jax.ShapeDtypeStruct(shape, BF16), weights),
        in_specs=[pl.BlockSpec(memory_space=pltpu.SMEM)]
        + [pl.BlockSpec((1,) + weight.shape[1:], lambda i: (i, 0, 0)) for weight in near + far]
        + [whole, whole],
        out_specs=(pl.BlockSpec(shape, lambda i: (0, 0, 0, 0, 0)), weights_block),
        scratch_shapes=[pltpu.VMEM((2 * rows, width), F32)] * 2,
        compiler_params=pltpu.CompilerParams(vmem_limit_bytes=32 * 1024 * 1024),
        cost_estimate=pl.CostEstimate(
            flops=16 * rows * chips * span * width,
            bytes_accessed=16 * chips * span * width + 8 * rows * features,
            transcendentals=0,
        ),
    )(place, *near, *far, rows_own, rows_in)


def attention_kernel(
    core_ref, both_ref, both_in_ref, far_ref, far_in_ref, _,
    early_ref, leave_ref, stay_ref, key_sum, value_sum,
):
    core = core_ref[0]
    first = core == 0
    blocks, _, _, rows, size = both_ref.shape
    count = blocks * rows
    near_ref, near_in_ref = both_ref.at[:, 1], both_in_ref.at[:, 1]

    def flat(value):
        return value.reshape(count, size)

    def in_order(mine, other):
        return jnp.where(first, mine, other), jnp.where(first, other, mine)

    query, grad = in_order(flat(both_ref[:, 0, core]), flat(both_in_ref[:, 0, core]))
    pairs = [
        in_order(flat(mine[:, of]), flat(theirs[:, of]))
        for mine, theirs in ((near_ref, near_in_ref), (far_ref, far_in_ref))
        for of in (core, 1 - core)
    ]
    keys = jnp.concatenate([pair[0] for pair in pairs], 0)
    values = jnp.concatenate([pair[1] for pair in pairs], 0)
    part = 2 * rows
    for block in range(count // part):
        here = slice(block * part, (block + 1) * part)
        outputs, grad_query, grad_key, grad_value = attention_block(
            query[here], grad[here], keys, values
        )
        cut = (2, rows, size)
        early_ref[2 * block : 2 * block + 2, 0] = outputs.reshape(cut)
        early_ref[2 * block : 2 * block + 2, 1] = grad_query.reshape(cut)
        if block == 0:
            key_sum[...] = grad_key
            value_sum[...] = grad_value
        else:
            key_sum[...] += grad_key
            value_sum[...] += grad_value
    for kind, total in enumerate((key_sum, value_sum)):
        for side in range(2):
            own = pl.ds(2 * side * count, count)
            other = pl.ds((2 * side + 1) * count, count)
            stay_ref[side, :, kind] = total[own, :].reshape(blocks, rows, size)
            leave_ref[side, :, kind] = total[other, :].reshape(blocks, rows, size).astype(BF16)


def attention(core, held, *operands):
    whole = pl.BlockSpec(memory_space=pltpu.VMEM)
    blocks, _, _, rows, size = operands[0].shape
    queries, keys = blocks * rows, 4 * blocks * rows
    return pl.pallas_call(
        attention_kernel,
        out_shape=(
            jax.ShapeDtypeStruct((blocks, 2, rows, size), BF16),
            jax.ShapeDtypeStruct((2, blocks, 2, rows, size), BF16),
            jax.ShapeDtypeStruct((2, blocks, 2, rows, size), F32),
        ),
        in_specs=[pl.BlockSpec(memory_space=pltpu.SMEM)]
        + [whole] * len(operands)
        + [pl.BlockSpec(memory_space=pl.ANY)] * len(held),
        out_specs=(whole,) * 3,
        scratch_shapes=[pltpu.VMEM((keys, size), F32)] * 2,
        compiler_params=pltpu.CompilerParams(vmem_limit_bytes=40 * 1024 * 1024),
        cost_estimate=pl.CostEstimate(
            flops=12 * queries * keys * size,
            bytes_accessed=8 * queries * size + 10 * keys * size,
            transcendentals=queries * keys,
        ),
    )(core, *operands, *held)


def pull_kernel(
    place_ref, back_ref, down_ref, weights_ref, weights_in_ref,
    states_ref, inverse_ref, gain_ref, up_ref, parcel_ref, part_sum, inner_sum,
):
    step = pl.program_id(0)
    groups, rows, _ = parcel_ref.shape
    width = gain_ref.shape[1]
    _, _, span, both = weights_ref.shape
    head_width = both // 2
    heads = head_width // HEAD_SIZE
    first, low_half = place_ref[0] == 0, place_ref[1] == 0
    here = pl.ds(pl.multiple_of(step * width, HEAD_SIZE), width)

    def by_token(kind):
        return jnp.concatenate([back_ref[head, kind] for head in range(heads)], 1)

    grad_query, grad_key, grad_value = by_token(1), by_token(2), by_token(3)
    own = jnp.where(first, grad_key, grad_value)
    other = jnp.where(first, grad_value, grad_key)
    left = jnp.concatenate([grad_query, own, other], 1)

    def right(side):
        mine, theirs = weights_ref[side, 0], weights_in_ref[side, 0]
        query_weight = jnp.where(first, mine[:, :head_width], theirs[:, :head_width])
        return jnp.concatenate([query_weight, mine[:, head_width:], theirs[:, head_width:]], 1)

    weight = jnp.concatenate([right(0), right(1)], 0)
    part = lax.dot_general(left, weight, ROWS_T, preferred_element_type=F32)
    near, far = part[:, :span], part[:, span:]
    part = jnp.concatenate(
        [jnp.where(low_half, near, far), jnp.where(low_half, far, near)], 1
    )
    part = part * gain_ref[...]
    unit = states_ref[:, here].astype(F32) * inverse_ref[...]
    inner = jnp.sum(part * unit, axis=-1, keepdims=True)
    part_sum[step] = part

    @pl.when(step == 0)
    def _():
        inner_sum[...] = inner

    @pl.when(step > 0)
    def _():
        inner_sum[...] += inner

    @pl.when(step == groups - 1)
    def _():
        scaled = inner_sum[...] * inverse_ref[...] * (1.0 / MODEL_WIDTH)
        rank = None
        for group in range(groups):
            columns = slice(group * width, (group + 1) * width)
            rest = part_sum[group] - states_ref[:, columns].astype(F32) * scaled
            rest = rest.astype(BF16)
            parcel_ref[group, :, :width] = rest
            term = lax.dot_general(rest, up_ref[:, columns], ROWS_T, preferred_element_type=F32)
            rank = term if rank is None else rank + term
        low_rank = jnp.dot(by_token(0), down_ref[...], preferred_element_type=F32)
        lane = lax.broadcasted_iota(jnp.int32, rank.shape, 1)
        extra = jnp.where(lane < HEAD_SIZE // 2, rank, low_rank).astype(BF16)
        for group in range(groups):
            parcel_ref[group, :, width:] = extra


def pull_back(place, back, down_padded, weights, weights_in, states, inverse, gain, up_padded):
    _, groups, span, both = weights.shape
    rows, features = states.shape
    width = features // groups
    whole = pl.BlockSpec(memory_space=pltpu.VMEM)
    return pl.pallas_call(
        pull_kernel,
        grid=(groups,),
        out_shape=jax.ShapeDtypeStruct((groups, rows, width + HEAD_SIZE), BF16),
        in_specs=[
            pl.BlockSpec(memory_space=pltpu.SMEM),
            pl.BlockSpec(back.shape, lambda i: (0, 0, 0, 0)),
            pl.BlockSpec(down_padded.shape, lambda i: (0, 0)),
        ]
        + [pl.BlockSpec((2, 1, span, both), lambda i: (0, i, 0, 0))] * 2
        + [
            pl.BlockSpec((rows, features), lambda i: (0, 0)),
            pl.BlockSpec((rows, 1), lambda i: (0, 0)),
            pl.BlockSpec((1, width), lambda i: (0, i)),
            pl.BlockSpec((HEAD_SIZE, features), lambda i: (0, 0)),
        ],
        out_specs=pl.BlockSpec((groups, rows, width + HEAD_SIZE), lambda i: (0, 0, 0)),
        scratch_shapes=[pltpu.VMEM((groups, rows, width), F32), pltpu.VMEM((rows, 1), F32)],
        compiler_params=pltpu.CompilerParams(vmem_limit_bytes=56 * 1024 * 1024),
        cost_estimate=pl.CostEstimate(
            flops=3 * rows * both * features,
            bytes_accessed=4 * features * both,
            transcendentals=0,
        ),
    )(place, back, down_padded, weights, weights_in, states, inverse, gain.reshape(1, features), up_padded)


def make_per_device(images, columns, groups):
    def per_device(
        states,
        adjoint,
        sampling_step_index,
        modulated_gain,
        query_weight,
        key_weight,
        value_weight,
        output_weight,
        down_factor,
        up_factor,
    ):
        is_first = lax.axis_index("c") == 0
        rows = states.shape[1]
        width = query_weight.shape[1]
        heads = width // HEAD_SIZE

        def in_order(mine, other, first):
            return jnp.where(first, mine, other), jnp.where(first, other, mine)

        place = [lax.axis_index("c"), lax.axis_index("yh"), lax.axis_index("img") % 2]
        place = jnp.stack(place).astype(jnp.int32)
        mine, other = pack(place, query_weight, key_weight, output_weight.T, value_weight)
        shard = jnp.concatenate(in_order(mine, swap(other, "c"), is_first), 0)
        far_shard = swap(shard, "yh")
        near = share(shard, "x", columns)

        def with_other_kind(weight):
            half = weight.shape[1] // 2
            ring = range(images)
            up = lax.ppermute(weight[:, :half], "img", [(i, (i + 1) % images) for i in ring])
            down = lax.ppermute(weight[:, half:], "img", [(i, (i - 1) % images) for i in ring])
            return weight, up, down

        inputs = states[0].astype(F32)
        inverse = lax.rsqrt(jnp.mean(inputs * inputs, axis=-1, keepdims=True) + 1e-06)
        unit_rows = inputs * inverse
        normed = (unit_rows * modulated_gain).astype(BF16)
        adjoint_low = adjoint[0].astype(BF16)
        rows_own = jnp.stack([normed, adjoint_low])
        rows_in = swap(rows_own, "c")
        far = share(far_shard, "x", columns)

        both, weights = project(
            place, with_other_kind(near), with_other_kind(far), rows_own, rows_in
        )
        weights_in = swap(weights, "c")
        both = trade(both, "x")
        far_like = swap(both[:, 1], "yh")
        early, leave, stay = attention(
            place, (weights_in,), both, swap(both, "c"), far_like, swap(far_like, "c")
        )

        stay = stay + swap(leave, "c").astype(F32)
        late = stay[0] + swap(stay[1].astype(BF16), "yh").astype(F32)
        back = trade(jnp.concatenate([early, late.astype(BF16)], 1), "x")
        outputs = back[:heads, 0].transpose(1, 0, 2).reshape(rows, width)

        rank = up_factor.shape[0]
        up_padded = jnp.pad(up_factor, ((0, HEAD_SIZE - rank), (0, 0)))
        down_padded = jnp.pad(down_factor, ((0, 0), (HEAD_SIZE - rank, 0)))
        local_width = MODEL_WIDTH // groups
        parcel = pull_back(
            place, back, down_padded, weights, weights_in, states[0], inverse, modulated_gain, up_padded
        )
        summed = jnp.sum(trade(parcel, "mdl").astype(F32), axis=0)
        adjoint_drift = inverse * summed[:, :local_width]
        drift_rank = inverse * summed[:, local_width : local_width + rank]
        rank_update = summed[:, -rank:].astype(BF16)

        first_column = lax.axis_index("mdl") * local_width
        adjoint_share = lax.dynamic_slice_in_dim(adjoint[0], first_column, local_width, 1)
        up_portion = lax.dynamic_slice_in_dim(up_factor, first_column, local_width, 1)
        time_now = (sampling_step_index[0].astype(F32) + 1.0) / (STEPS + 1.0)
        noise_level = jnp.sqrt(2.0 * time_now / (1.0 - time_now))
        adjoint_next = adjoint_share + adjoint_drift / STEPS
        drift_difference = jnp.dot(rank_update, up_portion, preferred_element_type=F32)
        match_residual = 2.0 / noise_level * drift_difference + noise_level * adjoint_next
        scaled_values = (2.0 / noise_level * match_residual).astype(BF16)
        up_term = lax.dot_general(rank_update, scaled_values, LEADING, preferred_element_type=F32)

        up_square = lax.dot_general(up_factor, up_factor, ROWS_T, preferred_element_type=F32)
        adjoint_rank = lax.dot_general(adjoint_low, up_factor, ROWS_T, preferred_element_type=F32)
        update_rank = jnp.dot(
            rank_update.astype(F32), up_square, precision=lax.Precision.HIGHEST
        )
        ratio = 2.0 / noise_level
        rank_backward = ratio * ratio * update_rank + 2.0 * (adjoint_rank + drift_rank / STEPS)
        down_term = lax.dot_general(
            rank_backward.astype(BF16), outputs, LEADING, preferred_element_type=F32
        )

        pieces = columns * 2
        table = jnp.concatenate([up_term, down_term], 1).astype(BF16)
        table = table.reshape(pieces, rank // pieces, local_width + width)
        piece = jnp.sum(trade(table, ("x", "c")).astype(F32), axis=0).astype(BF16)
        piece = share(piece, "img", images).astype(F32)
        piece = jnp.sum(piece, axis=0).astype(BF16)
        table = share(piece, SEQ, 2 * pieces).astype(F32)
        table = jnp.sum(table.reshape(columns, 2, 2, rank // pieces, -1), axis=1)
        table = table.reshape(rank, local_width + width)
        grad_up = table[:, :local_width]
        grad_down = table[:, local_width : local_width + width].T
        return (adjoint_drift[None], match_residual[None], grad_up, grad_down)

    return per_device


def build(mesh):
    images, seq, groups = (mesh.shape[name] for name in ("img", "seq", "mdl"))
    columns = seq // 4
    cut = Mesh(
        mesh.devices.reshape(images, columns, 2, 2, groups), ("img", "x", "yh", "c", "mdl")
    )
    return jax.shard_map(
        make_per_device(images, columns, groups),
        mesh=cut,
        in_specs=(
            P("img", SEQ, None),
            P("img", SEQ, None),
            P("img"),
            P(),
            P(SEQ, "mdl"),
            P(SEQ, "mdl"),
            P(SEQ, "mdl"),
            P("mdl", SEQ),
            P("mdl", None),
            P(),
        ),
        out_specs=(P("img", SEQ, "mdl"), P("img", SEQ, "mdl"), P(None, "mdl"), P("mdl", None)),
        check_vma=False,
    )


def solution(mesh):
    return build(mesh)
```

```python
import jax
import jax.numpy as jnp
from jax import lax
from jax.experimental import pallas as pl
from jax.experimental.pallas import tpu as pltpu
from jax.sharding import Mesh
from jax.sharding import PartitionSpec as P

MODEL_WIDTH = 3072
HEAD_SIZE = 128
STEPS = 28
SEQ = ("x", "yh", "c")
F32 = jnp.float32
BF16 = jnp.bfloat16
ROWS_T = (((1,), (1,)), ((), ()))
LEADING = (((0,), (0,)), ((), ()))


def swap(value, axis):
    return lax.ppermute(value, axis, [(0, 1), (1, 0)])


def trade(value, axis):
    return lax.all_to_all(value, axis, split_axis=0, concat_axis=0, tiled=True)


def share(value, axis, count):
    return trade(jnp.broadcast_to(value[None], (count,) + value.shape), axis)


def after(value, earlier):
    return value + 0 * earlier.reshape(-1)[0]


def attention_block(query, grad, keys, values):
    scale = HEAD_SIZE ** (-0.5)
    scores = lax.dot_general(query, keys, ROWS_T, preferred_element_type=F32) * scale
    row_max = jnp.max(scores, axis=-1, keepdims=True)
    weights = jnp.exp(scores - row_max)
    attend = weights * (1.0 / jnp.sum(weights, axis=-1, keepdims=True))
    attend_low = attend.astype(BF16)
    outputs = jnp.dot(attend_low, values, preferred_element_type=F32).astype(BF16)
    row_inner = jnp.sum(grad.astype(F32) * outputs.astype(F32), axis=-1, keepdims=True)
    grad_attend = lax.dot_general(grad, values, ROWS_T, preferred_element_type=F32)
    grad_scores = (attend * (grad_attend - row_inner)).astype(BF16)
    grad_query = jnp.dot(grad_scores, keys, preferred_element_type=F32) * scale
    grad_key = lax.dot_general(grad_scores, query, LEADING, preferred_element_type=F32) * scale
    grad_value = lax.dot_general(attend_low, grad, LEADING, preferred_element_type=F32)
    return outputs, grad_query.astype(BF16), grad_key, grad_value


def pack_kernel(place_ref, query_ref, key_ref, output_ref, value_ref, mine_ref, other_ref):
    first, even = place_ref[0] == 0, place_ref[2] == 0
    left = jnp.where(even, query_ref[...], key_ref[...])
    right = jnp.where(even, output_ref[...], value_ref[...])
    mine_ref[...] = jnp.where(first, left, right)
    other_ref[...] = jnp.where(first, right, left)


def pack(place, *weights):
    whole = pl.BlockSpec(memory_space=pltpu.VMEM)
    shape = jax.ShapeDtypeStruct(weights[0].shape, BF16)
    return pl.pallas_call(
        pack_kernel,
        out_shape=(shape, shape),
        in_specs=[pl.BlockSpec(memory_space=pltpu.SMEM)] + [whole] * len(weights),
        out_specs=(whole, whole),
        compiler_params=pltpu.CompilerParams(vmem_limit_bytes=56 * 1024 * 1024),
        cost_estimate=pl.CostEstimate(
            flops=0, bytes_accessed=12 * weights[0].size, transcendentals=0
        ),
    )(place, *weights)


def project_kernel(
    place_ref, near_ref, near_up_ref, near_down_ref, far_ref, far_up_ref, far_down_ref,
    rows_ref, rows_in_ref, out_ref, weights_ref, total, total_other,
):
    step = pl.program_id(0)
    first, half, even = place_ref[0] == 0, place_ref[1], place_ref[2] == 0
    _, span, width = near_ref.shape

    def in_order(mine, other):
        return jnp.where(even, mine, other), jnp.where(even, other, mine)

    def left(side):
        here = pl.ds(pl.multiple_of((2 * step + side) * span, HEAD_SIZE), span)
        own, other = rows_ref[0, :, here], rows_in_ref[0, :, here]
        rows = jnp.concatenate([jnp.where(first, own, other), jnp.where(first, other, own)], 0)
        adjoint = jnp.concatenate([rows_in_ref[1, :, here], rows_ref[1, :, here]], 0)
        return in_order(jnp.where(first, rows, adjoint), rows)

    near = near_ref[0], jnp.concatenate([near_up_ref[0], near_down_ref[0]], 0)
    far = far_ref[0], jnp.concatenate([far_up_ref[0], far_down_ref[0]], 0)
    for side, weights in enumerate((near, far)):
        one, two = in_order(*weights)
        weights_ref[side, 0, :, :width] = one
        weights_ref[side, 0, :, width:] = two
    near_left, far_left = left(half), left(1 - half)
    term, term_other = [
        jnp.dot(
            jnp.concatenate([near_left[kind], far_left[kind]], 1),
            jnp.concatenate([near[kind], far[kind]], 0),
            preferred_element_type=F32,
        )
        for kind in range(2)
    ]

    @pl.when(step == 0)
    def _():
        total[...] = term
        total_other[...] = term_other

    @pl.when(step > 0)
    def _():
        total[...] += term
        total_other[...] += term_other

    @pl.when(step == pl.num_programs(0) - 1)
    def _():
        chips, _, cores, rows, _ = out_ref.shape
        for kind, sums in enumerate(in_order(total[...], total_other[...])):
            low = sums.astype(BF16)
            for chip in range(chips):
                columns = slice(chip * HEAD_SIZE, (chip + 1) * HEAD_SIZE)
                for core in range(cores):
                    if chip * HEAD_SIZE < width:
                        piece = low[core * rows : (core + 1) * rows, columns]
                    else:
                        piece = jnp.zeros((rows, HEAD_SIZE), BF16)
                    out_ref[chip, kind, core] = piece


def project(place, near, far, rows_own, rows_in):
    _, rows, features = rows_own.shape
    chips, span, width = far[0].shape
    whole = pl.BlockSpec((2, rows, features), lambda i: (0, 0, 0))
    shape = (chips, 2, 2, rows, HEAD_SIZE)
    weights = jax.ShapeDtypeStruct((2, chips, span, 2 * width), BF16)
    weights_block = pl.BlockSpec((2, 1, span, 2 * width), lambda i: (0, i, 0, 0))
    return pl.pallas_call(
        project_kernel,
        grid=(chips,),
        out_shape=(jax.ShapeDtypeStruct(shape, BF16), weights),
        in_specs=[pl.BlockSpec(memory_space=pltpu.SMEM)]
        + [pl.BlockSpec((1,) + weight.shape[1:], lambda i: (i, 0, 0)) for weight in near + far]
        + [whole, whole],
        out_specs=(pl.BlockSpec(shape, lambda i: (0, 0, 0, 0, 0)), weights_block),
        scratch_shapes=[pltpu.VMEM((2 * rows, width), F32)] * 2,
        compiler_params=pltpu.CompilerParams(vmem_limit_bytes=32 * 1024 * 1024),
        cost_estimate=pl.CostEstimate(
            flops=16 * rows * chips * span * width,
            bytes_accessed=16 * chips * span * width + 8 * rows * features,
            transcendentals=0,
        ),
    )(place, *near, *far, rows_own, rows_in)


def attention_kernel(
    core_ref, both_ref, both_in_ref, far_ref, far_in_ref, _,
    early_ref, leave_ref, stay_ref, key_sum, value_sum,
):
    core = core_ref[0]
    first = core == 0
    blocks, _, _, rows, size = both_ref.shape
    count = blocks * rows
    near_ref, near_in_ref = both_ref.at[:, 1], both_in_ref.at[:, 1]

    def flat(value):
        return value.reshape(count, size)

    def in_order(mine, other):
        return jnp.where(first, mine, other), jnp.where(first, other, mine)

    query, grad = in_order(flat(both_ref[:, 0, core]), flat(both_in_ref[:, 0, core]))
    pairs = [
        in_order(flat(mine[:, of]), flat(theirs[:, of]))
        for mine, theirs in ((near_ref, near_in_ref), (far_ref, far_in_ref))
        for of in (core, 1 - core)
    ]
    keys = jnp.concatenate([pair[0] for pair in pairs], 0)
    values = jnp.concatenate([pair[1] for pair in pairs], 0)
    part = 2 * rows
    for block in range(count // part):
        here = slice(block * part, (block + 1) * part)
        outputs, grad_query, grad_key, grad_value = attention_block(
            query[here], grad[here], keys, values
        )
        cut = (2, rows, size)
        early_ref[2 * block : 2 * block + 2, 0] = outputs.reshape(cut)
        early_ref[2 * block : 2 * block + 2, 1] = grad_query.reshape(cut)
        if block == 0:
            key_sum[...] = grad_key
            value_sum[...] = grad_value
        else:
            key_sum[...] += grad_key
            value_sum[...] += grad_value
    for kind, total in enumerate((key_sum, value_sum)):
        for side in range(2):
            own = pl.ds(2 * side * count, count)
            other = pl.ds((2 * side + 1) * count, count)
            stay_ref[side, :, kind] = total[own, :].reshape(blocks, rows, size)
            leave_ref[side, :, kind] = total[other, :].reshape(blocks, rows, size).astype(BF16)


def attention(core, held, *operands):
    whole = pl.BlockSpec(memory_space=pltpu.VMEM)
    blocks, _, _, rows, size = operands[0].shape
    queries, keys = blocks * rows, 4 * blocks * rows
    return pl.pallas_call(
        attention_kernel,
        out_shape=(
            jax.ShapeDtypeStruct((blocks, 2, rows, size), BF16),
            jax.ShapeDtypeStruct((2, blocks, 2, rows, size), BF16),
            jax.ShapeDtypeStruct((2, blocks, 2, rows, size), F32),
        ),
        in_specs=[pl.BlockSpec(memory_space=pltpu.SMEM)]
        + [whole] * len(operands)
        + [pl.BlockSpec(memory_space=pl.ANY)] * len(held),
        out_specs=(whole,) * 3,
        scratch_shapes=[pltpu.VMEM((keys, size), F32)] * 2,
        compiler_params=pltpu.CompilerParams(vmem_limit_bytes=40 * 1024 * 1024),
        cost_estimate=pl.CostEstimate(
            flops=12 * queries * keys * size,
            bytes_accessed=8 * queries * size + 10 * keys * size,
            transcendentals=queries * keys,
        ),
    )(core, *operands, *held)


def pull_kernel(
    place_ref, back_ref, down_ref, weights_ref, weights_in_ref,
    states_ref, inverse_ref, gain_ref, up_ref, parcel_ref, part_sum, inner_sum,
):
    step = pl.program_id(0)
    groups, rows, _ = parcel_ref.shape
    width = gain_ref.shape[1]
    _, _, span, both = weights_ref.shape
    head_width = both // 2
    heads = head_width // HEAD_SIZE
    first, low_half = place_ref[0] == 0, place_ref[1] == 0
    here = pl.ds(pl.multiple_of(step * width, HEAD_SIZE), width)

    def by_token(kind):
        return jnp.concatenate([back_ref[head, kind] for head in range(heads)], 1)

    grad_query, grad_key, grad_value = by_token(1), by_token(2), by_token(3)
    own = jnp.where(first, grad_key, grad_value)
    other = jnp.where(first, grad_value, grad_key)
    left = jnp.concatenate([grad_query, own, other], 1)

    def right(side):
        mine, theirs = weights_ref[side, 0], weights_in_ref[side, 0]
        query_weight = jnp.where(first, mine[:, :head_width], theirs[:, :head_width])
        return jnp.concatenate([query_weight, mine[:, head_width:], theirs[:, head_width:]], 1)

    weight = jnp.concatenate([right(0), right(1)], 0)
    part = lax.dot_general(left, weight, ROWS_T, preferred_element_type=F32)
    near, far = part[:, :span], part[:, span:]
    part = jnp.concatenate(
        [jnp.where(low_half, near, far), jnp.where(low_half, far, near)], 1
    )
    part = part * gain_ref[...]
    unit = states_ref[:, here].astype(F32) * inverse_ref[...]
    inner = jnp.sum(part * unit, axis=-1, keepdims=True)
    part_sum[step] = part

    @pl.when(step == 0)
    def _():
        inner_sum[...] = inner

    @pl.when(step > 0)
    def _():
        inner_sum[...] += inner

    @pl.when(step == groups - 1)
    def _():
        scaled = inner_sum[...] * inverse_ref[...] * (1.0 / MODEL_WIDTH)
        rank = None
        for group in range(groups):
            columns = slice(group * width, (group + 1) * width)
            rest = part_sum[group] - states_ref[:, columns].astype(F32) * scaled
            rest = rest.astype(BF16)
            parcel_ref[group, :, :width] = rest
            term = lax.dot_general(rest, up_ref[:, columns], ROWS_T, preferred_element_type=F32)
            rank = term if rank is None else rank + term
        low_rank = jnp.dot(by_token(0), down_ref[...], preferred_element_type=F32)
        lane = lax.broadcasted_iota(jnp.int32, rank.shape, 1)
        extra = jnp.where(lane < HEAD_SIZE // 2, rank, low_rank).astype(BF16)
        for group in range(groups):
            parcel_ref[group, :, width:] = extra


def pull_back(place, back, down_padded, weights, weights_in, states, inverse, gain, up_padded):
    _, groups, span, both = weights.shape
    rows, features = states.shape
    width = features // groups
    whole = pl.BlockSpec(memory_space=pltpu.VMEM)
    return pl.pallas_call(
        pull_kernel,
        grid=(groups,),
        out_shape=jax.ShapeDtypeStruct((groups, rows, width + HEAD_SIZE), BF16),
        in_specs=[
            pl.BlockSpec(memory_space=pltpu.SMEM),
            pl.BlockSpec(back.shape, lambda i: (0, 0, 0, 0)),
            pl.BlockSpec(down_padded.shape, lambda i: (0, 0)),
        ]
        + [pl.BlockSpec((2, 1, span, both), lambda i: (0, i, 0, 0))] * 2
        + [
            pl.BlockSpec((rows, features), lambda i: (0, 0)),
            pl.BlockSpec((rows, 1), lambda i: (0, 0)),
            pl.BlockSpec((1, width), lambda i: (0, i)),
            pl.BlockSpec((HEAD_SIZE, features), lambda i: (0, 0)),
        ],
        out_specs=pl.BlockSpec((groups, rows, width + HEAD_SIZE), lambda i: (0, 0, 0)),
        scratch_shapes=[pltpu.VMEM((groups, rows, width), F32), pltpu.VMEM((rows, 1), F32)],
        compiler_params=pltpu.CompilerParams(vmem_limit_bytes=56 * 1024 * 1024),
        cost_estimate=pl.CostEstimate(
            flops=3 * rows * both * features,
            bytes_accessed=4 * features * both,
            transcendentals=0,
        ),
    )(place, back, down_padded, weights, weights_in, states, inverse, gain.reshape(1, features), up_padded)


def make_per_device(images, columns, groups):
    def per_device(
        states,
        adjoint,
        sampling_step_index,
        modulated_gain,
        query_weight,
        key_weight,
        value_weight,
        output_weight,
        down_factor,
        up_factor,
    ):
        is_first = lax.axis_index("c") == 0
        rows = states.shape[1]
        width = query_weight.shape[1]
        heads = width // HEAD_SIZE

        def in_order(mine, other, first):
            return jnp.where(first, mine, other), jnp.where(first, other, mine)

        place = [lax.axis_index("c"), lax.axis_index("yh"), lax.axis_index("img") % 2]
        place = jnp.stack(place).astype(jnp.int32)
        mine, other = pack(place, query_weight, key_weight, output_weight.T, value_weight)
        shard = jnp.concatenate(in_order(mine, swap(other, "c"), is_first), 0)
        far_shard = swap(shard, "yh")
        near = share(shard, "x", columns)

        def with_other_kind(weight):
            half = weight.shape[1] // 2
            ring = range(images)
            up = lax.ppermute(weight[:, :half], "img", [(i, (i + 1) % images) for i in ring])
            down = lax.ppermute(weight[:, half:], "img", [(i, (i - 1) % images) for i in ring])
            return weight, up, down

        inputs = states[0].astype(F32)
        inverse = lax.rsqrt(jnp.mean(inputs * inputs, axis=-1, keepdims=True) + 1e-06)
        unit_rows = inputs * inverse
        normed = (unit_rows * modulated_gain).astype(BF16)
        adjoint_low = adjoint[0].astype(BF16)
        rows_own = jnp.stack([after(normed, shard), adjoint_low])
        rows_in = swap(rows_own, "c")
        far = share(after(far_shard, rows_in), "x", columns)

        both, weights = project(
            place, with_other_kind(near), with_other_kind(far), rows_own, rows_in
        )
        weights_in = swap(weights, "c")
        both = trade(both, "x")
        far_like = swap(both[:, 1], "yh")
        early, leave, stay = attention(
            place, (weights_in,), both, swap(both, "c"), far_like, swap(far_like, "c")
        )

        stay = stay + swap(leave, "c").astype(F32)
        late = stay[0] + swap(stay[1].astype(BF16), "yh").astype(F32)
        back = trade(jnp.concatenate([early, late.astype(BF16)], 1), "x")
        outputs = back[:heads, 0].transpose(1, 0, 2).reshape(rows, width)

        rank = up_factor.shape[0]
        up_padded = jnp.pad(up_factor, ((0, HEAD_SIZE - rank), (0, 0)))
        down_padded = jnp.pad(down_factor, ((0, 0), (HEAD_SIZE - rank, 0)))
        local_width = MODEL_WIDTH // groups
        parcel = pull_back(
            place, back, down_padded, weights, weights_in, states[0], inverse, modulated_gain, up_padded
        )
        summed = jnp.sum(trade(parcel, "mdl").astype(F32), axis=0)
        adjoint_drift = inverse * summed[:, :local_width]
        drift_rank = inverse * summed[:, local_width : local_width + rank]
        rank_update = summed[:, -rank:].astype(BF16)

        first_column = lax.axis_index("mdl") * local_width
        adjoint_share = lax.dynamic_slice_in_dim(adjoint[0], first_column, local_width, 1)
        up_portion = lax.dynamic_slice_in_dim(up_factor, first_column, local_width, 1)
        time_now = (sampling_step_index[0].astype(F32) + 1.0) / (STEPS + 1.0)
        noise_level = jnp.sqrt(2.0 * time_now / (1.0 - time_now))
        adjoint_next = adjoint_share + adjoint_drift / STEPS
        drift_difference = jnp.dot(rank_update, up_portion, preferred_element_type=F32)
        match_residual = 2.0 / noise_level * drift_difference + noise_level * adjoint_next
        scaled_values = (2.0 / noise_level * match_residual).astype(BF16)
        up_term = lax.dot_general(rank_update, scaled_values, LEADING, preferred_element_type=F32)

        up_square = lax.dot_general(up_factor, up_factor, ROWS_T, preferred_element_type=F32)
        adjoint_rank = lax.dot_general(adjoint_low, up_factor, ROWS_T, preferred_element_type=F32)
        update_rank = jnp.dot(
            rank_update.astype(F32), up_square, precision=lax.Precision.HIGHEST
        )
        ratio = 2.0 / noise_level
        rank_backward = ratio * ratio * update_rank + 2.0 * (adjoint_rank + drift_rank / STEPS)
        down_term = lax.dot_general(
            rank_backward.astype(BF16), outputs, LEADING, preferred_element_type=F32
        )

        pieces = columns * 2
        table = jnp.concatenate([up_term, down_term], 1).astype(BF16)
        table = table.reshape(pieces, rank // pieces, local_width + width)
        piece = jnp.sum(trade(table, ("x", "c")).astype(F32), axis=0).astype(BF16)
        piece = share(piece, "img", images).astype(F32)
        piece = jnp.sum(piece, axis=0).astype(BF16)
        table = share(piece, SEQ, 2 * pieces).astype(F32)
        table = jnp.sum(table.reshape(columns, 2, 2, rank // pieces, -1), axis=1)
        table = table.reshape(rank, local_width + width)
        grad_up = table[:, :local_width]
        grad_down = table[:, local_width : local_width + width].T
        return (adjoint_drift[None], match_residual[None], grad_up, grad_down)

    return per_device


def build(mesh):
    images, seq, groups = (mesh.shape[name] for name in ("img", "seq", "mdl"))
    columns = seq // 4
    cut = Mesh(
        mesh.devices.reshape(images, columns, 2, 2, groups), ("img", "x", "yh", "c", "mdl")
    )
    return jax.shard_map(
        make_per_device(images, columns, groups),
        mesh=cut,
        in_specs=(
            P("img", SEQ, None),
            P("img", SEQ, None),
            P("img"),
            P(),
            P(SEQ, "mdl"),
            P(SEQ, "mdl"),
            P(SEQ, "mdl"),
            P("mdl", SEQ),
            P("mdl", None),
            P(),
        ),
        out_specs=(P("img", SEQ, "mdl"), P("img", SEQ, "mdl"), P(None, "mdl"), P("mdl", None)),
        check_vma=False,
    )


def solution(mesh):
    return build(mesh)
```

```python
import jax
import jax.numpy as jnp
from jax import lax
from jax.experimental import pallas as pl
from jax.experimental.pallas import tpu as pltpu
from jax.sharding import Mesh
from jax.sharding import PartitionSpec as P

MODEL_WIDTH = 3072
HEAD_SIZE = 128
STEPS = 28
LOG2_E = 1.4426950408889634
SEQ = ("x", "yh", "c")
F32 = jnp.float32
BF16 = jnp.bfloat16
ROWS_T = (((1,), (1,)), ((), ()))
LEADING = (((0,), (0,)), ((), ()))


def swap(value, axis):
    return lax.ppermute(value, axis, [(0, 1), (1, 0)])


def trade(value, axis):
    return lax.all_to_all(value, axis, split_axis=0, concat_axis=0, tiled=True)


def share(value, axis, count):
    return trade(jnp.broadcast_to(value[None], (count,) + value.shape), axis)


def after(value, earlier):
    return value + 0 * earlier.reshape(-1)[0]


def attention_block(query, grad, keys, values):
    scale = HEAD_SIZE ** (-0.5)
    scores = lax.dot_general(query, keys, ROWS_T, preferred_element_type=F32)
    row_max = jnp.max(scores, axis=-1, keepdims=True)
    weights = jnp.exp2((scores - row_max) * (scale * LOG2_E))
    attend = weights * (1.0 / jnp.sum(weights, axis=-1, keepdims=True))
    attend_low = attend.astype(BF16)
    outputs = jnp.dot(attend_low, values, preferred_element_type=F32).astype(BF16)
    row_inner = jnp.sum(grad.astype(F32) * outputs.astype(F32), axis=-1, keepdims=True)
    grad_attend = lax.dot_general(grad, values, ROWS_T, preferred_element_type=F32)
    grad_scores = (attend * (grad_attend - row_inner)).astype(BF16)
    grad_query = jnp.dot(grad_scores, keys, preferred_element_type=F32) * scale
    grad_key = lax.dot_general(grad_scores, query, LEADING, preferred_element_type=F32) * scale
    grad_value = lax.dot_general(attend_low, grad, LEADING, preferred_element_type=F32)
    return outputs, grad_query.astype(BF16), grad_key, grad_value


def pack_kernel(place_ref, query_ref, key_ref, output_ref, value_ref, mine_ref, other_ref):
    first, even = place_ref[0] == 0, place_ref[2] == 0
    left = jnp.where(even, query_ref[...], key_ref[...])
    right = jnp.where(even, output_ref[...], value_ref[...])
    mine_ref[...] = jnp.where(first, left, right)
    other_ref[...] = jnp.where(first, right, left)


def pack(place, *weights):
    whole = pl.BlockSpec(memory_space=pltpu.VMEM)
    shape = jax.ShapeDtypeStruct(weights[0].shape, BF16)
    return pl.pallas_call(
        pack_kernel,
        out_shape=(shape, shape),
        in_specs=[pl.BlockSpec(memory_space=pltpu.SMEM)] + [whole] * len(weights),
        out_specs=(whole, whole),
        compiler_params=pltpu.CompilerParams(vmem_limit_bytes=56 * 1024 * 1024),
        cost_estimate=pl.CostEstimate(
            flops=0, bytes_accessed=12 * weights[0].size, transcendentals=0
        ),
    )(place, *weights)


def project_kernel(
    place_ref, near_ref, near_up_ref, near_down_ref, far_ref, far_up_ref, far_down_ref,
    rows_ref, rows_in_ref, out_ref, weights_ref, total, total_other,
):
    step = pl.program_id(0)
    first, half, even = place_ref[0] == 0, place_ref[1], place_ref[2] == 0
    _, span, width = near_ref.shape

    def in_order(mine, other):
        return jnp.where(even, mine, other), jnp.where(even, other, mine)

    def left(side):
        here = pl.ds(pl.multiple_of((2 * step + side) * span, HEAD_SIZE), span)
        own, other = rows_ref[0, :, here], rows_in_ref[0, :, here]
        rows = jnp.concatenate([jnp.where(first, own, other), jnp.where(first, other, own)], 0)
        adjoint = jnp.concatenate([rows_in_ref[1, :, here], rows_ref[1, :, here]], 0)
        return in_order(jnp.where(first, rows, adjoint), rows)

    near = near_ref[0], jnp.concatenate([near_up_ref[0], near_down_ref[0]], 0)
    far = far_ref[0], jnp.concatenate([far_up_ref[0], far_down_ref[0]], 0)
    for side, weights in enumerate((near, far)):
        one, two = in_order(*weights)
        weights_ref[side, 0, :, :width] = one
        weights_ref[side, 0, :, width:] = two
    near_left, far_left = left(half), left(1 - half)
    term, term_other = [
        jnp.dot(
            jnp.concatenate([near_left[kind], far_left[kind]], 1),
            jnp.concatenate([near[kind], far[kind]], 0),
            preferred_element_type=F32,
        )
        for kind in range(2)
    ]

    @pl.when(step == 0)
    def _():
        total[...] = term
        total_other[...] = term_other

    @pl.when(step > 0)
    def _():
        total[...] += term
        total_other[...] += term_other

    @pl.when(step == pl.num_programs(0) - 1)
    def _():
        chips, _, cores, rows, _ = out_ref.shape
        for kind, sums in enumerate(in_order(total[...], total_other[...])):
            low = sums.astype(BF16)
            for chip in range(chips):
                columns = slice(chip * HEAD_SIZE, (chip + 1) * HEAD_SIZE)
                for core in range(cores):
                    if chip * HEAD_SIZE < width:
                        piece = low[core * rows : (core + 1) * rows, columns]
                    else:
                        piece = jnp.zeros((rows, HEAD_SIZE), BF16)
                    out_ref[chip, kind, core] = piece


def project(place, near, far, rows_own, rows_in):
    _, rows, features = rows_own.shape
    chips, span, width = far[0].shape
    whole = pl.BlockSpec((2, rows, features), lambda i: (0, 0, 0))
    shape = (chips, 2, 2, rows, HEAD_SIZE)
    weights = jax.ShapeDtypeStruct((2, chips, span, 2 * width), BF16)
    weights_block = pl.BlockSpec((2, 1, span, 2 * width), lambda i: (0, i, 0, 0))
    return pl.pallas_call(
        project_kernel,
        grid=(chips,),
        out_shape=(jax.ShapeDtypeStruct(shape, BF16), weights),
        in_specs=[pl.BlockSpec(memory_space=pltpu.SMEM)]
        + [pl.BlockSpec((1,) + weight.shape[1:], lambda i: (i, 0, 0)) for weight in near + far]
        + [whole, whole],
        out_specs=(pl.BlockSpec(shape, lambda i: (0, 0, 0, 0, 0)), weights_block),
        scratch_shapes=[pltpu.VMEM((2 * rows, width), F32)] * 2,
        compiler_params=pltpu.CompilerParams(vmem_limit_bytes=32 * 1024 * 1024),
        cost_estimate=pl.CostEstimate(
            flops=16 * rows * chips * span * width,
            bytes_accessed=16 * chips * span * width + 8 * rows * features,
            transcendentals=0,
        ),
    )(place, *near, *far, rows_own, rows_in)


def attention_kernel(
    core_ref, both_ref, both_in_ref, far_ref, far_in_ref, _,
    early_ref, leave_ref, stay_ref, key_sum, value_sum,
):
    core = core_ref[0]
    first = core == 0
    blocks, _, _, rows, size = both_ref.shape
    count = blocks * rows
    near_ref, near_in_ref = both_ref.at[:, 1], both_in_ref.at[:, 1]

    def flat(value):
        return value.reshape(count, size)

    def in_order(mine, other):
        return jnp.where(first, mine, other), jnp.where(first, other, mine)

    query, grad = in_order(flat(both_ref[:, 0, core]), flat(both_in_ref[:, 0, core]))
    pairs = [
        in_order(flat(mine[:, of]), flat(theirs[:, of]))
        for mine, theirs in ((near_ref, near_in_ref), (far_ref, far_in_ref))
        for of in (core, 1 - core)
    ]
    keys = jnp.concatenate([pair[0] for pair in pairs], 0)
    values = jnp.concatenate([pair[1] for pair in pairs], 0)
    outputs, grad_query, *sums = attention_block(query, grad, keys, values)
    early_ref[:, 0] = outputs.reshape(blocks, rows, size)
    early_ref[:, 1] = grad_query.reshape(blocks, rows, size)
    key_sum[...], value_sum[...] = sums
    for kind, total in enumerate((key_sum, value_sum)):
        for side in range(2):
            own = pl.ds(2 * side * count, count)
            other = pl.ds((2 * side + 1) * count, count)
            stay_ref[side, :, kind] = total[own, :].reshape(blocks, rows, size)
            leave_ref[side, :, kind] = total[other, :].reshape(blocks, rows, size).astype(BF16)


def attention(core, held, *operands):
    whole = pl.BlockSpec(memory_space=pltpu.VMEM)
    blocks, _, _, rows, size = operands[0].shape
    queries, keys = blocks * rows, 4 * blocks * rows
    return pl.pallas_call(
        attention_kernel,
        out_shape=(
            jax.ShapeDtypeStruct((blocks, 2, rows, size), BF16),
            jax.ShapeDtypeStruct((2, blocks, 2, rows, size), BF16),
            jax.ShapeDtypeStruct((2, blocks, 2, rows, size), F32),
        ),
        in_specs=[pl.BlockSpec(memory_space=pltpu.SMEM)]
        + [whole] * len(operands)
        + [pl.BlockSpec(memory_space=pl.ANY)] * len(held),
        out_specs=(whole,) * 3,
        scratch_shapes=[pltpu.VMEM((keys, size), F32)] * 2,
        compiler_params=pltpu.CompilerParams(vmem_limit_bytes=40 * 1024 * 1024),
        cost_estimate=pl.CostEstimate(
            flops=12 * queries * keys * size,
            bytes_accessed=8 * queries * size + 10 * keys * size,
            transcendentals=queries * keys,
        ),
    )(core, *operands, *held)


def pull_kernel(
    place_ref, back_ref, down_ref, weights_ref, weights_in_ref,
    states_ref, inverse_ref, gain_ref, up_ref, parcel_ref, part_sum, inner_sum,
):
    step = pl.program_id(0)
    groups, rows, _ = parcel_ref.shape
    width = gain_ref.shape[1]
    _, _, span, both = weights_ref.shape
    head_width = both // 2
    heads = head_width // HEAD_SIZE
    first, low_half = place_ref[0] == 0, place_ref[1] == 0
    here = pl.ds(pl.multiple_of(step * width, HEAD_SIZE), width)

    def by_token(kind):
        return jnp.concatenate([back_ref[head, kind] for head in range(heads)], 1)

    grad_query, grad_key, grad_value = by_token(1), by_token(2), by_token(3)
    own = jnp.where(first, grad_key, grad_value)
    other = jnp.where(first, grad_value, grad_key)
    left = jnp.concatenate([grad_query, own, other], 1)

    def right(side):
        mine, theirs = weights_ref[side, 0], weights_in_ref[side, 0]
        query_weight = jnp.where(first, mine[:, :head_width], theirs[:, :head_width])
        return jnp.concatenate([query_weight, mine[:, head_width:], theirs[:, head_width:]], 1)

    weight = jnp.concatenate([right(0), right(1)], 0)
    part = lax.dot_general(left, weight, ROWS_T, preferred_element_type=F32)
    near, far = part[:, :span], part[:, span:]
    part = jnp.concatenate(
        [jnp.where(low_half, near, far), jnp.where(low_half, far, near)], 1
    )
    part = part * gain_ref[...]
    unit = states_ref[:, here].astype(F32) * inverse_ref[...]
    inner = jnp.sum(part * unit, axis=-1, keepdims=True)
    part_sum[step] = part

    @pl.when(step == 0)
    def _():
        inner_sum[...] = inner

    @pl.when(step > 0)
    def _():
        inner_sum[...] += inner

    @pl.when(step == groups - 1)
    def _():
        scaled = inner_sum[...] * inverse_ref[...] * (1.0 / MODEL_WIDTH)
        rank = None
        for group in range(groups):
            columns = slice(group * width, (group + 1) * width)
            rest = part_sum[group] - states_ref[:, columns].astype(F32) * scaled
            rest = rest.astype(BF16)
            parcel_ref[group, :, :width] = rest
            term = lax.dot_general(rest, up_ref[:, columns], ROWS_T, preferred_element_type=F32)
            rank = term if rank is None else rank + term
        low_rank = jnp.dot(by_token(0), down_ref[...], preferred_element_type=F32)
        lane = lax.broadcasted_iota(jnp.int32, rank.shape, 1)
        extra = jnp.where(lane < HEAD_SIZE // 2, rank, low_rank).astype(BF16)
        for group in range(groups):
            parcel_ref[group, :, width:] = extra


def pull_back(place, back, down_padded, weights, weights_in, states, inverse, gain, up_padded):
    _, groups, span, both = weights.shape
    rows, features = states.shape
    width = features // groups
    whole = pl.BlockSpec(memory_space=pltpu.VMEM)
    return pl.pallas_call(
        pull_kernel,
        grid=(groups,),
        out_shape=jax.ShapeDtypeStruct((groups, rows, width + HEAD_SIZE), BF16),
        in_specs=[
            pl.BlockSpec(memory_space=pltpu.SMEM),
            pl.BlockSpec(back.shape, lambda i: (0, 0, 0, 0)),
            pl.BlockSpec(down_padded.shape, lambda i: (0, 0)),
        ]
        + [pl.BlockSpec((2, 1, span, both), lambda i: (0, i, 0, 0))] * 2
        + [
            pl.BlockSpec((rows, features), lambda i: (0, 0)),
            pl.BlockSpec((rows, 1), lambda i: (0, 0)),
            pl.BlockSpec((1, width), lambda i: (0, i)),
            pl.BlockSpec((HEAD_SIZE, features), lambda i: (0, 0)),
        ],
        out_specs=pl.BlockSpec((groups, rows, width + HEAD_SIZE), lambda i: (0, 0, 0)),
        scratch_shapes=[pltpu.VMEM((groups, rows, width), F32), pltpu.VMEM((rows, 1), F32)],
        compiler_params=pltpu.CompilerParams(vmem_limit_bytes=56 * 1024 * 1024),
        cost_estimate=pl.CostEstimate(
            flops=3 * rows * both * features,
            bytes_accessed=4 * features * both,
            transcendentals=0,
        ),
    )(place, back, down_padded, weights, weights_in, states, inverse, gain.reshape(1, features), up_padded)


def make_per_device(images, columns, groups):
    def per_device(
        states,
        adjoint,
        sampling_step_index,
        modulated_gain,
        query_weight,
        key_weight,
        value_weight,
        output_weight,
        down_factor,
        up_factor,
    ):
        is_first = lax.axis_index("c") == 0
        rows = states.shape[1]
        width = query_weight.shape[1]
        heads = width // HEAD_SIZE

        def in_order(mine, other, first):
            return jnp.where(first, mine, other), jnp.where(first, other, mine)

        place = [lax.axis_index("c"), lax.axis_index("yh"), lax.axis_index("img") % 2]
        place = jnp.stack(place).astype(jnp.int32)
        mine, other = pack(place, query_weight, key_weight, output_weight.T, value_weight)
        shard = jnp.concatenate(in_order(mine, swap(other, "c"), is_first), 0)
        far_shard = swap(shard, "yh")
        near = share(shard, "x", columns)

        def with_other_kind(weight):
            half = weight.shape[1] // 2
            ring = range(images)
            up = lax.ppermute(weight[:, :half], "img", [(i, (i + 1) % images) for i in ring])
            down = lax.ppermute(weight[:, half:], "img", [(i, (i - 1) % images) for i in ring])
            return weight, up, down

        inputs = states[0].astype(F32)
        inverse = lax.rsqrt(jnp.mean(inputs * inputs, axis=-1, keepdims=True) + 1e-06)
        unit_rows = inputs * inverse
        normed = (unit_rows * modulated_gain).astype(BF16)
        adjoint_low = adjoint[0].astype(BF16)
        rows_own = jnp.stack([normed, adjoint_low])
        rows_in = swap(rows_own, "c")
        far = share(after(far_shard, rows_in), "x", columns)

        both, weights = project(
            place, with_other_kind(near), with_other_kind(far), rows_own, rows_in
        )
        weights_in = swap(weights, "c")
        both = trade(both, "x")
        far_like = swap(both[:, 1], "yh")
        early, leave, stay = attention(
            place, (weights_in,), both, swap(both, "c"), far_like, swap(far_like, "c")
        )

        stay = stay + swap(leave, "c").astype(F32)
        late = stay[0] + swap(stay[1].astype(BF16), "yh").astype(F32)
        back = trade(jnp.concatenate([early, late.astype(BF16)], 1), "x")
        outputs = back[:heads, 0].transpose(1, 0, 2).reshape(rows, width)

        rank = up_factor.shape[0]
        up_padded = jnp.pad(up_factor, ((0, HEAD_SIZE - rank), (0, 0)))
        down_padded = jnp.pad(down_factor, ((0, 0), (HEAD_SIZE - rank, 0)))
        local_width = MODEL_WIDTH // groups
        parcel = pull_back(
            place, back, down_padded, weights, weights_in, states[0], inverse, modulated_gain, up_padded
        )
        summed = jnp.sum(trade(parcel, "mdl").astype(F32), axis=0)
        adjoint_drift = inverse * summed[:, :local_width]
        drift_rank = inverse * summed[:, local_width : local_width + rank]
        rank_update = summed[:, -rank:].astype(BF16)

        first_column = lax.axis_index("mdl") * local_width
        adjoint_share = lax.dynamic_slice_in_dim(adjoint[0], first_column, local_width, 1)
        up_portion = lax.dynamic_slice_in_dim(up_factor, first_column, local_width, 1)
        time_now = (sampling_step_index[0].astype(F32) + 1.0) / (STEPS + 1.0)
        noise_level = jnp.sqrt(2.0 * time_now / (1.0 - time_now))
        adjoint_next = adjoint_share + adjoint_drift / STEPS
        drift_difference = jnp.dot(rank_update, up_portion, preferred_element_type=F32)
        match_residual = 2.0 / noise_level * drift_difference + noise_level * adjoint_next
        scaled_values = (2.0 / noise_level * match_residual).astype(BF16)
        up_term = lax.dot_general(rank_update, scaled_values, LEADING, preferred_element_type=F32)

        up_square = lax.dot_general(up_factor, up_factor, ROWS_T, preferred_element_type=F32)
        adjoint_rank = lax.dot_general(adjoint_low, up_factor, ROWS_T, preferred_element_type=F32)
        update_rank = jnp.dot(
            rank_update.astype(F32), up_square, precision=lax.Precision.HIGHEST
        )
        ratio = 2.0 / noise_level
        rank_backward = ratio * ratio * update_rank + 2.0 * (adjoint_rank + drift_rank / STEPS)
        down_term = lax.dot_general(
            rank_backward.astype(BF16), outputs, LEADING, preferred_element_type=F32
        )

        pieces = columns * 2
        table = jnp.concatenate([up_term, down_term], 1).astype(BF16)
        table = table.reshape(pieces, rank // pieces, local_width + width)
        piece = jnp.sum(trade(table, ("x", "c")).astype(F32), axis=0).astype(BF16)
        piece = share(piece, "img", images).astype(F32)
        piece = jnp.sum(piece, axis=0).astype(BF16)
        table = share(piece, SEQ, 2 * pieces).astype(F32)
        table = jnp.sum(table.reshape(columns, 2, 2, rank // pieces, -1), axis=1)
        table = table.reshape(rank, local_width + width)
        grad_up = table[:, :local_width]
        grad_down = table[:, local_width : local_width + width].T
        return (adjoint_drift[None], match_residual[None], grad_up, grad_down)

    return per_device


def build(mesh):
    images, seq, groups = (mesh.shape[name] for name in ("img", "seq", "mdl"))
    columns = seq // 4
    cut = Mesh(
        mesh.devices.reshape(images, columns, 2, 2, groups), ("img", "x", "yh", "c", "mdl")
    )
    return jax.shard_map(
        make_per_device(images, columns, groups),
        mesh=cut,
        in_specs=(
            P("img", SEQ, None),
            P("img", SEQ, None),
            P("img"),
            P(),
            P(SEQ, "mdl"),
            P(SEQ, "mdl"),
            P(SEQ, "mdl"),
            P("mdl", SEQ),
            P("mdl", None),
            P(),
        ),
        out_specs=(P("img", SEQ, "mdl"), P("img", SEQ, "mdl"), P(None, "mdl"), P("mdl", None)),
        check_vma=False,
    )


def solution(mesh):
    return build(mesh)
```
